32 devices in a mesh: space: 8 (over y, x, core), rep: 4 (over z).
Axes of the slice: x: 2, y: 2, z: 4, core: 2. Of those that a mesh axis runs over, the one named last changes fastest.
Arguments:
- leaf_density: bfloat16 [888, 8192], P(None, 'space'), may hold values from -6 to 6
- upward_ops: bfloat16 [8, 888, 888], P(None, 'rep'), may hold values from -0.0625 to 0.0625
- far_ops: bfloat16 [12, 888, 888], P('rep'), may hold values from -0.0625 to 0.0625
- downward_ops: bfloat16 [8, 888, 888], P(None, 'rep'), may hold values from -0.1875 to 0.1875
- fine_lists: int32 [12, 8192], P('rep', 'space'), may hold values from 0 to 3071
- coarse_lists: int32 [12, 1024], P('rep', 'space'), may hold values from 0 to 383
Outputs:
- local_check: bfloat16 [888, 8192], P('rep', 'space')
The draws below stay inside these ranges and needn't reach their ends.
Inputs may be any that keep to these rules, and one draw needn't show every extreme that they name: `fine_lists`: entry k of box g names a box of the previous subtree (below 1024), of its own (below 2048) or of the next one; indices outside the grid of subtrees read zeros. `coarse_lists`: entry k of coarse box p names a coarse box of the previous coarse subtree (below 128), of its own (below 256) or of the next one; indices outside the grid read zeros.
All inputs are finite; a program needn't handle non-finite values.
Results may differ from the reference program's by a relative error of at most 0.013.
Values may be sent and summed in bfloat16 or wider, within the bound.
A program may use at most 128 MiB of HBM per device.

```python
import jax
import jax.numpy as jnp

DENS = 888
SLOTS = 12
BOX_DEV = 1024
FINE = 8192
COARSE = 1024


def place_ends(entries, own_key, least, high):
    longest = entries.shape.index(max(entries.shape))
    spots = []
    for shift in (0, 1):
        where = [jax.random.randint(jax.random.fold_in(own_key, axis), (), 0, length) for axis, length in enumerate(entries.shape)]
        where[longest] = (where[longest] + shift) % entries.shape[longest]
        spots.append(tuple(where))
    return entries.at[spots[0]].set(least).at[spots[1]].set(high)


def levels(stream_key, extent, pieces, smallest, high):
    factor_of, own = 1.0, jax.random.fold_in(stream_key, 6)
    for position, shards_of in pieces:
        draws = jnp.exp(jax.random.uniform(jax.random.fold_in(own, position), (shards_of,), jnp.float32, smallest / len(pieces), high / len(pieces)))
        factor_of = factor_of * jnp.repeat(draws, extent[position] // shards_of).reshape([-1 if axis == position else 1 for axis in range(len(extent))])
    return factor_of


def bell_draw(own_key, dims, width, limit, pieces=(), held_as=jnp.bfloat16):
    drawn = jax.random.normal(own_key, dims, jnp.float32) * width
    if len(pieces) > 0:
        drawn = levels(own_key, dims, pieces, -0.22, 0.18) * drawn
    return jnp.clip(drawn, min=-limit, max=limit).astype(held_as)


def setup_inputs(seed: int = 0) -> dict:
    streams_of = jax.random.split(jax.random.key(seed), 7)
    return {
        "leaf_density": bell_draw(streams_of[0], (DENS, FINE), 1.0, 6.0, ((1, 8),)),
        "upward_ops": bell_draw(streams_of[1], (8, DENS, DENS), (8 * DENS) ** -0.5, 0.0625, ((1, 4),)),
        "far_ops": bell_draw(streams_of[2], (SLOTS, DENS, DENS), (SLOTS * DENS) ** -0.5, 0.0625, ((0, 4),)),
        "downward_ops": bell_draw(streams_of[3], (8, DENS, DENS), DENS ** -0.5, 0.1875, ((1, 4),)),
        "fine_lists": place_ends(jax.random.randint(streams_of[4], (SLOTS, FINE), 0, 3 * BOX_DEV), jax.random.fold_in(streams_of[4], 1), 0, (3 * BOX_DEV) - 1).astype(jnp.int32),
        "coarse_lists": place_ends(jax.random.randint(streams_of[5], (SLOTS, COARSE), 0, 3 * (BOX_DEV // 8)), jax.random.fold_in(streams_of[5], 1), 0, (3 * (BOX_DEV // 8)) - 1).astype(jnp.int32),
    }


coarse_scale = 0.5


def reference(leaf_density, upward_ops, far_ops, downward_ops, fine_lists, coarse_lists):
    density_rows = leaf_density.shape[0]
    fine_total = leaf_density.shape[1]
    coarse_total = fine_total // 8
    coarse_block = BOX_DEV // 8
    children = leaf_density.reshape(density_rows, coarse_total, 8).astype(jnp.float32)
    parents = jnp.einsum("crq,qpc->rp", upward_ops.astype(jnp.float32), children)
    coarse_up = parents.astype(jnp.bfloat16)
    padded = jnp.pad(leaf_density, ((0, 0), (BOX_DEV, BOX_DEV)))
    padded_up = jnp.pad(coarse_up, ((0, 0), (coarse_block, coarse_block)))
    anchor = (jnp.arange(fine_total, dtype=jnp.int32) // BOX_DEV) * BOX_DEV
    coarse_anchor = (jnp.arange(coarse_total, dtype=jnp.int32) // coarse_block) * coarse_block
    fine_check = jnp.zeros((density_rows, fine_total), jnp.float32)
    coarse_sum = jnp.zeros((density_rows, coarse_total), jnp.float32)
    for offset in range(SLOTS):
        sources = jnp.take(padded, (anchor + fine_lists[offset]).astype(jnp.int32), axis=1)
        fine_check = fine_check + jnp.dot(far_ops[offset], sources, preferred_element_type=jnp.float32)
        remote = jnp.take(padded_up, (coarse_anchor + coarse_lists[offset]).astype(jnp.int32), axis=1)
        coarse_sum = coarse_sum + jnp.dot(far_ops[offset], remote, preferred_element_type=jnp.float32)
    coarse_check = (coarse_scale * coarse_sum).astype(jnp.bfloat16)
    spread = jnp.einsum("crq,qp->rpc", downward_ops.astype(jnp.float32), coarse_check.astype(jnp.float32))
    return (fine_check + spread.reshape(density_rows, fine_total)).astype(jnp.bfloat16)
```

```python
import functools

import jax
import jax.numpy as jnp
from jax import lax
from jax.experimental import pallas as pl
from jax.experimental.pallas import tpu as pltpu
from jax.sharding import PartitionSpec as P

coarse_scale = 0.5
F32, BF16 = jnp.float32, jnp.bfloat16
VM = pltpu.VMEM
PARAMS = pltpu.CompilerParams(vmem_limit_bytes=48 * 2**20)


def whole(count):
    return [pl.BlockSpec(memory_space=VM) for _ in range(count)]


def dot(a, b):
    return jnp.dot(a, b, preferred_element_type=F32)


def one_hot(row, first, count):
    spots = lax.broadcasted_iota(jnp.int32, (count, row.shape[1]), 0) + first
    return jnp.where(spots == row, 1.0, 0.0).astype(BF16)


def upward_kernel(density, ops, out):
    children, parents = ops.shape[0], out.shape[1]
    boxes = density.shape[1]
    total = jnp.zeros(out.shape, F32)
    for child in range(children):
        box = lax.broadcasted_iota(jnp.int32, (boxes, parents), 0)
        parent = lax.broadcasted_iota(jnp.int32, (boxes, parents), 1)
        pick = jnp.where(box == parent * children + child, 1.0, 0.0).astype(BF16)
        total += dot(ops[child], dot(density[...], pick).astype(BF16))
    out[...] = total.astype(BF16)


def own_kernel(lists, density, out):
    boxes = density.shape[1]
    out[...] = dot(density[...], one_hot(lists[0], boxes, boxes)).astype(BF16)


def far_kernel(lists, before, after, picked, ops, out):
    boxes = before.shape[1]
    total = jnp.zeros((ops.shape[1], out.shape[2]), F32)
    for entry in range(ops.shape[0]):
        row = lists[entry]
        sources = picked[entry].astype(F32)
        sources += dot(before[...], one_hot(row, 0, boxes))
        sources += dot(after[...], one_hot(row, 2 * boxes, boxes))
        total += dot(ops[entry], sources.astype(BF16))
    block = out.shape[1]
    for owner in range(out.shape[0]):
        out[owner] = total[owner * block:(owner + 1) * block].astype(BF16)


def coarse_kernel(lists, before, own, after, ops, out):
    boxes = own.shape[1]
    total = jnp.zeros(out.shape, F32)
    for entry in range(ops.shape[0]):
        row = lists[entry]
        sources = dot(own[...], one_hot(row, boxes, boxes))
        sources += dot(before[...], one_hot(row, 0, boxes))
        sources += dot(after[...], one_hot(row, 2 * boxes, boxes))
        total += dot(ops[entry], sources.astype(BF16))
    out[...] = (coarse_scale * total).astype(BF16)


def downward_kernel(check, ops, fine, out):
    children, parents = ops.shape[0], check.shape[1]
    boxes = out.shape[1]
    total = fine[...].astype(F32)
    for child in range(children):
        term = dot(ops[child], check[...])
        high = term.astype(BF16)
        low = (term - high.astype(F32)).astype(BF16)
        parent = lax.broadcasted_iota(jnp.int32, (parents, boxes), 0)
        box = lax.broadcasted_iota(jnp.int32, (parents, boxes), 1)
        place = jnp.where(box == parent * children + child, 1.0, 0.0).astype(BF16)
        total += dot(high, place) + dot(low, place)
    out[...] = total.astype(BF16)


def local(leaf_density, upward_ops, far_ops, downward_ops, fine_lists, coarse_lists):
    rows, boxes = leaf_density.shape
    children, own_rows, _ = upward_ops.shape
    parents = boxes // children
    slots = far_ops.shape[0]
    wide = 256 if boxes % 256 == 0 else boxes
    peers = lax.axis_size("space")
    up = [(i, i + 1) for i in range(peers - 1)]
    down = [(j, i) for i, j in up]
    before = lax.ppermute(leaf_density, "space", up)
    after = lax.ppermute(leaf_density, "space", down)
    fine3 = fine_lists.reshape(slots, 1, boxes)
    coarse3 = coarse_lists.reshape(slots, 1, parents)

    up_rows = pl.pallas_call(
        upward_kernel,
        out_shape=jax.ShapeDtypeStruct((own_rows, parents), BF16),
        in_specs=whole(2), out_specs=whole(1)[0], compiler_params=PARAMS,
        cost_estimate=pl.CostEstimate(
            flops=2 * rows * boxes * (boxes + own_rows), bytes_accessed=6 * 2**20, transcendentals=0),
    )(leaf_density, upward_ops)
    stacked = lax.all_gather(up_rows, "rep", axis=0, tiled=True)
    coarse_before = lax.ppermute(stacked, "space", up)
    coarse_after = lax.ppermute(stacked, "space", down)

    picked = pl.pallas_call(
        own_kernel,
        grid=(slots, boxes // wide),
        out_shape=jax.ShapeDtypeStruct((slots, rows, boxes), BF16),
        in_specs=[
            pl.BlockSpec((1, 1, wide), lambda k, c: (k, 0, c)),
            pl.BlockSpec((rows, boxes), lambda k, c: (0, 0)),
        ],
        out_specs=pl.BlockSpec((None, rows, wide), lambda k, c: (k, 0, c)),
        compiler_params=PARAMS,
        cost_estimate=pl.CostEstimate(
            flops=2 * rows * boxes * boxes * slots, bytes_accessed=8 * 2**20, transcendentals=0),
    )(fine3, leaf_density)

    coarse_partial = pl.pallas_call(
        coarse_kernel,
        out_shape=jax.ShapeDtypeStruct((rows, parents), BF16),
        in_specs=whole(5), out_specs=whole(1)[0], compiler_params=PARAMS,
        cost_estimate=pl.CostEstimate(
            flops=2 * rows * parents * slots * (3 * parents + rows),
            bytes_accessed=6 * 2**20, transcendentals=0),
    )(coarse3, coarse_before, stacked, coarse_after, far_ops)
    coarse_check = lax.psum(coarse_partial, "rep")

    fine_partial = pl.pallas_call(
        far_kernel,
        grid=(boxes // wide,),
        out_shape=jax.ShapeDtypeStruct((rows // own_rows, own_rows, boxes), BF16),
        in_specs=[
            pl.BlockSpec((slots, 1, wide), lambda c: (0, 0, c)),
            pl.BlockSpec((rows, boxes), lambda c: (0, 0)),
            pl.BlockSpec((rows, boxes), lambda c: (0, 0)),
            pl.BlockSpec((slots, rows, wide), lambda c: (0, 0, c)),
            pl.BlockSpec((slots, rows, rows), lambda c: (0, 0, 0)),
        ],
        out_specs=pl.BlockSpec((rows // own_rows, own_rows, wide), lambda c: (0, 0, c)),
        compiler_params=PARAMS,
        cost_estimate=pl.CostEstimate(
            flops=2 * rows * boxes * slots * (2 * boxes + rows),
            bytes_accessed=16 * 2**20, transcendentals=0),
    )(fine3, before, after, picked, far_ops)
    fine_check = lax.psum_scatter(fine_partial, "rep", scatter_dimension=0, tiled=False)

    return pl.pallas_call(
        downward_kernel,
        out_shape=jax.ShapeDtypeStruct((own_rows, boxes), BF16),
        in_specs=whole(3), out_specs=whole(1)[0], compiler_params=PARAMS,
    )(coarse_check, downward_ops, fine_check)


def solution(mesh):
    return jax.shard_map(
        local,
        mesh=mesh,
        in_specs=(
            P(None, "space"),
            P(None, "rep", None),
            P("rep", None, None),
            P(None, "rep", None),
            P("rep", "space"),
            P("rep", "space"),
        ),
        out_specs=P("rep", "space"),
        check_vma=False,
    )
```

```python
import functools

import jax
import jax.numpy as jnp
from jax import lax
from jax.experimental import pallas as pl
from jax.experimental.pallas import tpu as pltpu
from jax.sharding import PartitionSpec as P

coarse_scale = 0.5
F32, BF16 = jnp.float32, jnp.bfloat16
MESH = pl.DeviceIdType.MESH


def dot(a, b):
    return jnp.dot(a, b, preferred_element_type=F32)


def remote(src, dst, send, recv, device):
    return pltpu.make_async_remote_copy(
        src_ref=src, dst_ref=dst, send_sem=send, recv_sem=recv, device_id=device, device_id_type=MESH)


def one_hot(row, count, ramp):
    step = ramp.shape[0]
    pieces = []
    for first in range(0, count, step):
        spot = (row - first).astype(F32).astype(BF16)
        pieces.append(jnp.where(ramp == spot, jnp.ones((), BF16), jnp.zeros((), BF16)))
    return pieces


def stack(pieces):
    return pieces[0] if len(pieces) == 1 else jnp.concatenate(pieces, axis=0)


def blocks_of(total, count, block, held):
    spare = jnp.zeros((held, total.shape[1]), F32)
    total = jnp.concatenate([total, spare], axis=0)
    return [total[j * block:j * block + held] for j in range(count)]


def kernel(spaces, reps, wide, block,
           density_hbm, up_hbm, far_hbm, down_hbm, lists, coarse_lists, out,
           density, near, far, up_ops, far_ops, down_ops, picked, ramp_ref,
           sums, right, left, gathered, coarse_here, coarse_window, coarse_sums, coarse_right, coarse_left,
           checks, full, high, low, spread,
           load_sem, window_send, window_recv, cw_send, cw_recv, ag_send, ag_recv, ck_send, ck_recv,
           rs_send, rs_recv, ls_send, ls_recv, crs_send, crs_recv, cls_send, cls_recv):
    s, z = lax.axis_index("space"), lax.axis_index("rep")
    rows, boxes = density.shape
    slots = far_ops.shape[0]
    children = up_ops.shape[0]
    parents = boxes // children
    chunks = boxes // wide
    held = sums.shape[2]
    parity = lax.rem(s, 2)
    mate = s + 1 - 2 * parity
    other = s - 1 + 2 * parity
    has_other = jnp.logical_and(other >= 0, other < spaces)

    loads = [
        pltpu.make_async_copy(src, dst, load_sem.at[i])
        for i, (src, dst) in enumerate(
            [(density_hbm, density), (up_hbm, up_ops), (far_hbm, far_ops), (down_hbm, down_ops)])
    ]
    for copy in loads:
        copy.start()

    barrier = pltpu.get_barrier_semaphore()
    for d in range(1, reps):
        pl.semaphore_signal(barrier, inc=1, device_id=(s, lax.rem(z + d, reps)), device_id_type=MESH)
    pl.semaphore_signal(barrier, inc=1, device_id=(mate, z), device_id_type=MESH)

    @pl.when(has_other)
    def _():
        pl.semaphore_signal(barrier, inc=1, device_id=(other, z), device_id_type=MESH)

    ramp_ref[...] = lax.broadcasted_iota(jnp.int32, ramp_ref.shape, 0).astype(F32).astype(BF16)
    pl.semaphore_wait(barrier, reps + has_other.astype(jnp.int32))

    to_far = remote(density_hbm, far, window_send.at[0], window_recv.at[0], (other, z))
    to_near = remote(density_hbm, near, window_send.at[1], window_recv.at[1], (mate, z))

    @pl.when(has_other)
    def _():
        to_far.start()

    to_near.start()

    @pl.when(jnp.logical_not(has_other))
    def _():
        far[...] = jnp.zeros(far.shape, BF16)
        coarse_window[:, 2 * parents:] = jnp.zeros((coarse_window.shape[0], parents), BF16)

    loads[0].wait()
    loads[1].wait()
    total = jnp.zeros((block, parents), F32)
    for child in range(0, children, 2):
        column = lax.broadcasted_iota(jnp.int32, (1, 2 * parents), 1)
        source = jnp.where(
            column < parents, column * children + child, (column - parents) * children + child + 1)
        pair = dot(density[...], stack(one_hot(source, boxes, ramp_ref[:, :2 * parents]))).astype(BF16)
        total += dot(up_ops[child], pair[:, :parents])
        total += dot(up_ops[child + 1], pair[:, parents:])
    gathered[z] = jnp.concatenate([total, jnp.zeros((held - block, parents), F32)], axis=0).astype(BF16)

    def gather_copies(buffer, send, recv):
        return [
            remote(buffer.at[z], buffer.at[z], send.at[d - 1], recv.at[d - 1], (s, lax.rem(z + d, reps)))
            for d in range(1, reps)
        ]

    up_copies = gather_copies(gathered, ag_send, ag_recv)
    for copy in up_copies:
        copy.start()

    def assemble(buffer):
        for j in range(reps):
            full[j * block:(j + 1) * block, :] = buffer[j][:block].astype(F32)
        return full[...].astype(BF16)

    own_base = boxes
    near_base = 2 * boxes * (1 - parity)
    far_base = 2 * boxes * parity
    to_near.wait_recv()

    def pick(chunk, _):
        columns = pl.ds(pl.multiple_of(chunk * wide, wide), wide)
        ramp = ramp_ref[...]
        for entry in range(slots):
            row = lists[entry:entry + 1, columns]
            values = dot(density[...], stack(one_hot(row - own_base, boxes, ramp)))
            values += dot(near[...], stack(one_hot(row - near_base, boxes, ramp)))
            picked[entry, :, columns] = values.astype(BF16)
        return 0

    first_part = chunks // 2
    lax.fori_loop(0, first_part, pick, 0)

    for copy in up_copies:
        copy.wait_recv()
    coarse_here[...] = jnp.concatenate(
        [assemble(gathered), jnp.zeros((coarse_here.shape[0] - rows, parents), BF16)], axis=0)
    coarse_window[:, :parents] = coarse_here[...]
    coarse_near = remote(
        coarse_here, coarse_window.at[:, pl.ds(parents, parents)], cw_send.at[0], cw_recv.at[0], (mate, z))
    coarse_far = remote(
        coarse_here, coarse_window.at[:, pl.ds(2 * parents, parents)], cw_send.at[1], cw_recv.at[1], (other, z))
    coarse_near.start()

    @pl.when(has_other)
    def _():
        coarse_far.start()

    lax.fori_loop(first_part, chunks, pick, 0)

    loads[2].wait()
    coarse_near.wait_recv()

    @pl.when(has_other)
    def _():
        coarse_far.wait_recv()

    total = jnp.zeros((rows, parents), F32)
    ramp = lax.broadcasted_iota(jnp.int32, (parents, parents), 0)
    for entry in range(slots):
        row = coarse_lists[entry:entry + 1, :]
        place = [
            jnp.where(ramp == row - base, 1.0, 0.0).astype(BF16)
            for base in (own_base // children, near_base // children, far_base // children)
        ]
        values = dot(coarse_window[:rows, :], stack(place))
        total += dot(far_ops[entry], values.astype(BF16))
    for j, value in enumerate(blocks_of(coarse_scale * total, reps, block, held)):
        coarse_sums[0, j] = value.astype(BF16)

    @pl.when(has_other)
    def _():
        to_far.wait_recv()

    def move_right(chunk, ways, j):
        _, buffer, _, send, recv, _, _ = ways
        return remote(buffer.at[chunk, j], buffer.at[chunk, j], send.at[chunk, j], recv.at[chunk, j], (s, z + 1))

    def move_left(chunk, ways, j):
        _, _, buffer, _, _, send, recv = ways
        return remote(buffer.at[chunk, j], buffer.at[chunk, j], send.at[chunk, j], recv.at[chunk, j], (s, z - 1))

    def forward_right(chunk, ways):
        mine, buffer = ways[0], ways[1]
        for j in reversed(range(1, reps)):
            @pl.when(j > z)
            def _(j=j):
                copy = move_right(chunk, ways, j)

                @pl.when(z > 0)
                def _():
                    copy.wait_recv()
                    buffer[chunk, j] = (buffer[chunk, j].astype(F32) + mine[chunk, j].astype(F32)).astype(BF16)

                @pl.when(z == 0)
                def _():
                    buffer[chunk, j] = mine[chunk, j]

                copy.start()

    def forward_left(chunk, ways):
        mine, buffer = ways[0], ways[2]
        for j in range(reps - 1):
            @pl.when(j < z)
            def _(j=j):
                copy = move_left(chunk, ways, j)

                @pl.when(z < reps - 1)
                def _():
                    copy.wait_recv()
                    buffer[chunk, j] = (buffer[chunk, j].astype(F32) + mine[chunk, j].astype(F32)).astype(BF16)

                @pl.when(z == reps - 1)
                def _():
                    buffer[chunk, j] = mine[chunk, j]

                copy.start()

    def finished(chunk, ways):
        mine, go_right, go_left = ways[:3]

        @pl.when(z > 0)
        def _():
            move_right(chunk, ways, z).wait_recv()

        @pl.when(z == 0)
        def _():
            go_right[chunk, z] = jnp.zeros(go_right.shape[2:], BF16)

        @pl.when(z < reps - 1)
        def _():
            move_left(chunk, ways, z).wait_recv()

        @pl.when(z == reps - 1)
        def _():
            go_left[chunk, z] = jnp.zeros(go_left.shape[2:], BF16)

        return mine[chunk, z].astype(F32) + go_right[chunk, z].astype(F32) + go_left[chunk, z].astype(F32)

    def settle(chunk, ways):
        for j in range(reps):
            @pl.when(j > z)
            def _(j=j):
                move_right(chunk, ways, j).wait_send()

            @pl.when(j < z)
            def _(j=j):
                move_left(chunk, ways, j).wait_send()

    fine_ways = (sums, right, left, rs_send, rs_recv, ls_send, ls_recv)
    coarse_ways = (coarse_sums, coarse_right, coarse_left, crs_send, crs_recv, cls_send, cls_recv)

    def step(t):
        @pl.when(t == z)
        def _():
            forward_right(0, coarse_ways)

        @pl.when(t == reps - 1 - z)
        def _():
            forward_left(0, coarse_ways)

        @pl.when(jnp.logical_and(t >= z, t - z < chunks))
        def _():
            forward_right(t - z, fine_ways)

        back = reps - 1 - z

        @pl.when(jnp.logical_and(t >= back, t - back < chunks))
        def _():
            forward_left(t - back, fine_ways)

    def translate(t, _):
        columns = pl.ds(pl.multiple_of(t * wide, wide), wide)
        ramp = ramp_ref[...]
        total = jnp.zeros((rows, wide), F32)
        for entry in range(slots):
            row = lists[entry:entry + 1, columns]
            values = dot(far[...], stack(one_hot(row - far_base, boxes, ramp)))
            values += picked[entry, :, columns].astype(F32)
            total += dot(far_ops[entry], values.astype(BF16))
        for j, value in enumerate(blocks_of(total, reps, block, held)):
            sums[t, j] = value.astype(BF16)
        step(t)
        return 0

    lax.fori_loop(0, chunks, translate, 0)

    check_copies = gather_copies(checks, ck_send, ck_recv)
    for t in range(chunks, chunks + reps - 1):
        step(t)
        if t == max(chunks, reps - 1):
            checks[z] = finished(0, coarse_ways).astype(BF16)
            for copy in check_copies:
                copy.start()

    loads[3].wait()
    for copy in check_copies:
        copy.wait_recv()
    check = assemble(checks)
    for child in range(children):
        term = dot(down_ops[child], check)
        top = term.astype(BF16)
        columns = pl.ds(child * parents, parents)
        high[:, columns] = top
        low[:, columns] = (term - top.astype(F32)).astype(BF16)

    def place(chunk, _):
        columns = pl.ds(pl.multiple_of(chunk * wide, wide), wide)
        parent = lax.broadcasted_iota(jnp.int32, (parents, wide), 0) * children
        box = lax.broadcasted_iota(jnp.int32, (parents, wide), 1) + chunk * wide
        spots = stack([
            jnp.where(parent == box - child, 1.0, 0.0).astype(BF16) for child in range(children)
        ])
        spread[:, columns] = dot(high[...], spots) + dot(low[...], spots)
        return 0

    lax.fori_loop(0, chunks, place, 0)

    def finish(chunk, _):
        columns = pl.ds(pl.multiple_of(chunk * wide, wide), wide)
        out[:, columns] = (finished(chunk, fine_ways)[:block] + spread[:, columns]).astype(BF16)
        settle(chunk, fine_ways)
        return 0

    lax.fori_loop(0, chunks, finish, 0)
    settle(0, coarse_ways)
    for copy in up_copies + check_copies + [to_near, coarse_near]:
        copy.wait_send()

    @pl.when(has_other)
    def _():
        to_far.wait_send()
        coarse_far.wait_send()


def local(spaces, reps, leaf_density, upward_ops, far_ops, downward_ops, fine_lists, coarse_lists):
    rows, boxes = leaf_density.shape
    children, block, _ = upward_ops.shape
    slots = far_ops.shape[0]
    parents = boxes // children
    wide = 256 if boxes % 256 == 0 else boxes
    chunks = boxes // wide
    held = -(-block // 16) * 16
    padded = -(-rows // 16) * 16
    vm, dma = pltpu.VMEM, pltpu.SemaphoreType.DMA
    anywhere = pl.BlockSpec(memory_space=pl.ANY)
    inside = pl.BlockSpec(memory_space=vm)
    moving = vm((chunks, reps, held, wide), BF16)
    coarse_moving = vm((1, reps, held, parents), BF16)
    return pl.pallas_call(
        functools.partial(kernel, spaces, reps, wide, block),
        out_shape=jax.ShapeDtypeStruct((block, boxes), BF16),
        in_specs=[anywhere] * 4 + [inside] * 2,
        out_specs=inside,
        scratch_shapes=[
            vm((rows, boxes), BF16), vm((rows, boxes), BF16), vm((rows, boxes), BF16),
            vm(upward_ops.shape, BF16), vm(far_ops.shape, BF16), vm(downward_ops.shape, BF16),
            vm((slots, rows, boxes), BF16), vm((min(256, boxes), wide), BF16),
            moving, moving, moving,
            vm((reps, held, parents), BF16), vm((padded, parents), BF16), vm((padded, 3 * parents), BF16),
            coarse_moving, coarse_moving, coarse_moving,
            vm((reps, held, parents), BF16), vm((rows, parents), F32),
            vm((block, boxes), BF16), vm((block, boxes), BF16), vm((block, boxes), F32),
            dma((4,)), dma((2,)), dma((2,)), dma((2,)), dma((2,)),
            dma((reps - 1,)), dma((reps - 1,)), dma((reps - 1,)), dma((reps - 1,)),
        ] + [dma((chunks, reps))] * 4 + [dma((1, reps))] * 4,
        compiler_params=pltpu.CompilerParams(
            collective_id=0, has_side_effects=True, vmem_limit_bytes=56 * 2**20),
    )(leaf_density, upward_ops, far_ops, downward_ops, fine_lists, coarse_lists)


def solution(mesh):
    return jax.shard_map(
        functools.partial(local, mesh.shape["space"], mesh.shape["rep"]),
        mesh=mesh,
        in_specs=(
            P(None, "space"),
            P(None, "rep", None),
            P("rep", None, None),
            P(None, "rep", None),
            P("rep", "space"),
            P("rep", "space"),
        ),
        out_specs=P("rep", "space"),
        check_vma=False,
    )
```

```python
import functools

import jax
import jax.numpy as jnp
from jax import lax
from jax.experimental import pallas as pl
from jax.experimental.pallas import tpu as pltpu
from jax.sharding import PartitionSpec as P

coarse_scale = 0.5
F32, BF16 = jnp.float32, jnp.bfloat16
MESH = pl.DeviceIdType.MESH


def dot(a, b):
    return jnp.dot(a, b, preferred_element_type=F32)


def remote(src, dst, send, recv, device):
    return pltpu.make_async_remote_copy(
        src_ref=src, dst_ref=dst, send_sem=send, recv_sem=recv, device_id=device, device_id_type=MESH)


def one_hot(row, count, ramp):
    step = ramp.shape[0]
    pieces = []
    for first in range(0, count, step):
        spot = (row - first).astype(F32).astype(BF16)
        pieces.append(jnp.where(ramp == spot, jnp.ones((), BF16), jnp.zeros((), BF16)))
    return pieces


def stack(pieces):
    return pieces[0] if len(pieces) == 1 else jnp.concatenate(pieces, axis=0)


def blocks_of(total, count, block, held):
    spare = jnp.zeros((held, total.shape[1]), F32)
    total = jnp.concatenate([total, spare], axis=0)
    return [total[j * block:j * block + held] for j in range(count)]


def kernel(spaces, reps, wide, piece, block,
           density_hbm, up_hbm, far_hbm, down_hbm, lists, coarse_lists, out,
           density, near, far, up_raw, far_ops, down_raw, ops, wide_rows, picked, ramp_ref,
           sums, right, left, gathered, coarse_here, coarse_window, coarse_sums, coarse_right, coarse_left,
           checks, full, high, low, spread,
           load_sem, window_send, window_recv, sp_send, sp_recv, cw_send, cw_recv, ag_send, ag_recv, ck_send, ck_recv,
           rs_send, rs_recv, ls_send, ls_recv, crs_send, crs_recv, cls_send, cls_recv):
    s, z = lax.axis_index("space"), lax.axis_index("rep")
    rows, boxes = density.shape
    slots = far_ops.shape[0]
    children = ops.shape[0]
    parents = boxes // children
    chunks = boxes // wide
    held = sums.shape[2]
    parity = lax.rem(s, 2)
    mate = s + 1 - 2 * parity
    other = s - 1 + 2 * parity
    has_other = jnp.logical_and(other >= 0, other < spaces)

    loads = [
        pltpu.make_async_copy(src, dst, load_sem.at[i])
        for i, (src, dst) in enumerate(
            [(density_hbm, density), (up_hbm, up_raw), (far_hbm, far_ops), (down_hbm, down_raw)])
    ]
    for copy in loads:
        copy.start()

    barrier = pltpu.get_barrier_semaphore()
    for d in range(1, reps):
        pl.semaphore_signal(barrier, inc=1, device_id=(s, lax.rem(z + d, reps)), device_id_type=MESH)
    pl.semaphore_signal(barrier, inc=1, device_id=(mate, z), device_id_type=MESH)

    @pl.when(has_other)
    def _():
        pl.semaphore_signal(barrier, inc=1, device_id=(other, z), device_id_type=MESH)

    ramp_ref[...] = lax.broadcasted_iota(jnp.int32, ramp_ref.shape, 0).astype(F32).astype(BF16)
    pl.semaphore_wait(barrier, reps + has_other.astype(jnp.int32))

    def share(owner):
        return pl.ds(pl.multiple_of(owner * piece, piece), piece)

    rest = pl.ds(reps * piece, boxes - reps * piece)
    to_near = remote(density_hbm, near, window_send.at[0], window_recv.at[0], (mate, z))
    to_share = remote(density_hbm.at[:, share(z)], far.at[:, share(z)],
                      window_send.at[1], window_recv.at[1], (other, z))
    to_rest = remote(density_hbm.at[:, rest], far.at[:, rest], window_send.at[2], window_recv.at[2], (other, z))
    spread_copies = [
        remote(far.at[:, share(z)], far.at[:, share(z)], sp_send.at[d - 1], sp_recv.at[d - 1],
               (s, lax.rem(z + d, reps)))
        for d in range(1, reps)
    ]

    @pl.when(has_other)
    def _():
        to_share.start()
        to_rest.start()

    to_near.start()

    @pl.when(jnp.logical_not(has_other))
    def _():
        far[...] = jnp.zeros(far.shape, BF16)
        coarse_window[:, 2 * parents:] = jnp.zeros((coarse_window.shape[0], parents), BF16)

    def by_child(raw):
        lanes = wide_rows.shape[2]
        for part in range(wide_rows.shape[0]):
            low_end, high_end = part * lanes, min(rows, (part + 1) * lanes)
            span = high_end - low_end
            wide_rows[part, :block * children, :span] = raw[:, low_end:high_end].astype(F32)
            for child in range(children):
                mine = wide_rows[part, pl.ds(child, block, stride=children), :]
                ops[child, :, low_end:high_end] = mine[:, :span].astype(BF16)

    loads[0].wait()
    loads[1].wait()
    by_child(up_raw)
    total = jnp.zeros((block, parents), F32)
    for child in range(0, children, 2):
        column = lax.broadcasted_iota(jnp.int32, (1, 2 * parents), 1)
        source = jnp.where(
            column < parents, column * children + child, (column - parents) * children + child + 1)
        pair = dot(density[...], stack(one_hot(source, boxes, ramp_ref[:, :2 * parents]))).astype(BF16)
        total += dot(ops[child], pair[:, :parents])
        total += dot(ops[child + 1], pair[:, parents:])
    gathered[z] = jnp.concatenate([total, jnp.zeros((held - block, parents), F32)], axis=0).astype(BF16)

    def gather_copies(buffer, send, recv):
        return [
            remote(buffer.at[z], buffer.at[z], send.at[d - 1], recv.at[d - 1], (s, lax.rem(z + d, reps)))
            for d in range(1, reps)
        ]

    up_copies = gather_copies(gathered, ag_send, ag_recv)
    for copy in up_copies:
        copy.start()

    @pl.when(has_other)
    def _():
        to_share.wait_recv()
        for copy in spread_copies:
            copy.start()

    def assemble(buffer):
        for j in range(reps):
            full[j * block:(j + 1) * block, :] = buffer[j][:block].astype(F32)
        return full[...].astype(BF16)

    own_base = boxes
    near_base = 2 * boxes * (1 - parity)
    far_base = 2 * boxes * parity
    to_near.wait_recv()

    def pick(chunk, _):
        columns = pl.ds(pl.multiple_of(chunk * wide, wide), wide)
        ramp = ramp_ref[...]
        for entry in range(slots):
            row = lists[entry:entry + 1, columns]
            values = dot(density[...], stack(one_hot(row - own_base, boxes, ramp)))
            values += dot(near[...], stack(one_hot(row - near_base, boxes, ramp)))
            picked[entry, :, columns] = values.astype(BF16)
        return 0

    first_part = 1
    lax.fori_loop(0, first_part, pick, 0)

    for copy in up_copies:
        copy.wait_recv()
    coarse_here[...] = jnp.concatenate(
        [assemble(gathered), jnp.zeros((coarse_here.shape[0] - rows, parents), BF16)], axis=0)
    coarse_window[:, :parents] = coarse_here[...]
    coarse_near = remote(
        coarse_here, coarse_window.at[:, pl.ds(parents, parents)], cw_send.at[0], cw_recv.at[0], (mate, z))
    coarse_far = remote(
        coarse_here, coarse_window.at[:, pl.ds(2 * parents, parents)], cw_send.at[1], cw_recv.at[1], (other, z))
    coarse_near.start()

    @pl.when(has_other)
    def _():
        coarse_far.start()

    lax.fori_loop(first_part, chunks, pick, 0)

    loads[2].wait()
    coarse_near.wait_recv()

    @pl.when(has_other)
    def _():
        coarse_far.wait_recv()

    total = jnp.zeros((rows, parents), F32)
    ramp = lax.broadcasted_iota(jnp.int32, (parents, parents), 0)
    for entry in range(slots):
        row = coarse_lists[entry:entry + 1, :]
        place = [
            jnp.where(ramp == row - base, 1.0, 0.0).astype(BF16)
            for base in (own_base // children, near_base // children, far_base // children)
        ]
        values = dot(coarse_window[:rows, :], stack(place))
        total += dot(far_ops[entry], values.astype(BF16))
    for j, value in enumerate(blocks_of(coarse_scale * total, reps, block, held)):
        coarse_sums[0, j] = value.astype(BF16)

    def move_right(chunk, ways, j):
        _, buffer, _, send, recv, _, _ = ways
        return remote(buffer.at[chunk, j], buffer.at[chunk, j], send.at[chunk, j], recv.at[chunk, j], (s, z + 1))

    def move_left(chunk, ways, j):
        _, _, buffer, _, _, send, recv = ways
        return remote(buffer.at[chunk, j], buffer.at[chunk, j], send.at[chunk, j], recv.at[chunk, j], (s, z - 1))

    def forward_right(chunk, ways):
        mine, buffer = ways[0], ways[1]
        for j in reversed(range(1, reps)):
            @pl.when(j > z)
            def _(j=j):
                copy = move_right(chunk, ways, j)

                @pl.when(z > 0)
                def _():
                    copy.wait_recv()
                    buffer[chunk, j] = (buffer[chunk, j].astype(F32) + mine[chunk, j].astype(F32)).astype(BF16)

                @pl.when(z == 0)
                def _():
                    buffer[chunk, j] = mine[chunk, j]

                copy.start()

    def forward_left(chunk, ways):
        mine, buffer = ways[0], ways[2]
        for j in range(reps - 1):
            @pl.when(j < z)
            def _(j=j):
                copy = move_left(chunk, ways, j)

                @pl.when(z < reps - 1)
                def _():
                    copy.wait_recv()
                    buffer[chunk, j] = (buffer[chunk, j].astype(F32) + mine[chunk, j].astype(F32)).astype(BF16)

                @pl.when(z == reps - 1)
                def _():
                    buffer[chunk, j] = mine[chunk, j]

                copy.start()

    def finished(chunk, ways):
        mine, go_right, go_left = ways[:3]

        @pl.when(z > 0)
        def _():
            move_right(chunk, ways, z).wait_recv()

        @pl.when(z == 0)
        def _():
            go_right[chunk, z] = jnp.zeros(go_right.shape[2:], BF16)

        @pl.when(z < reps - 1)
        def _():
            move_left(chunk, ways, z).wait_recv()

        @pl.when(z == reps - 1)
        def _():
            go_left[chunk, z] = jnp.zeros(go_left.shape[2:], BF16)

        return mine[chunk, z].astype(F32) + go_right[chunk, z].astype(F32) + go_left[chunk, z].astype(F32)

    def settle(chunk, ways):
        for j in range(reps):
            @pl.when(j > z)
            def _(j=j):
                move_right(chunk, ways, j).wait_send()

            @pl.when(j < z)
            def _(j=j):
                move_left(chunk, ways, j).wait_send()

    fine_ways = (sums, right, left, rs_send, rs_recv, ls_send, ls_recv)
    coarse_ways = (coarse_sums, coarse_right, coarse_left, crs_send, crs_recv, cls_send, cls_recv)

    def coarse_step(t):
        @pl.when(t == z)
        def _():
            forward_right(0, coarse_ways)

        @pl.when(t == reps - 1 - z)
        def _():
            forward_left(0, coarse_ways)

    def step(t):
        coarse_step(t + 1)

        @pl.when(jnp.logical_and(t >= z, t - z < chunks))
        def _():
            forward_right(t - z, fine_ways)

        back = reps - 1 - z

        @pl.when(jnp.logical_and(t >= back, t - back < chunks))
        def _():
            forward_left(t - back, fine_ways)

    def translate(t, _):
        columns = pl.ds(pl.multiple_of(t * wide, wide), wide)
        ramp = ramp_ref[...]
        total = jnp.zeros((rows, wide), F32)
        for entry in range(slots):
            row = lists[entry:entry + 1, columns]
            values = dot(far[...], stack(one_hot(row - far_base, boxes, ramp)))
            values += picked[entry, :, columns].astype(F32)
            total += dot(far_ops[entry], values.astype(BF16))
        for j, value in enumerate(blocks_of(total, reps, block, held)):
            sums[t, j] = value.astype(BF16)
        step(t)
        return 0

    coarse_step(0)

    @pl.when(has_other)
    def _():
        to_rest.wait_recv()
        for copy in spread_copies:
            copy.wait_recv()

    lax.fori_loop(0, chunks, translate, 0)

    check_copies = gather_copies(checks, ck_send, ck_recv)
    for t in range(chunks, chunks + reps - 1):
        step(t)
        if t == max(chunks, reps - 1):
            checks[z] = finished(0, coarse_ways).astype(BF16)
            for copy in check_copies:
                copy.start()
            loads[3].wait()
            by_child(down_raw)

    for copy in check_copies:
        copy.wait_recv()
    check = assemble(checks)
    for child in range(children):
        term = dot(ops[child], check)
        top = term.astype(BF16)
        columns = pl.ds(child * parents, parents)
        high[:, columns] = top
        low[:, columns] = (term - top.astype(F32)).astype(BF16)

    def place(chunk, _):
        columns = pl.ds(pl.multiple_of(chunk * wide, wide), wide)
        parent = lax.broadcasted_iota(jnp.int32, (parents, wide), 0) * children
        box = lax.broadcasted_iota(jnp.int32, (parents, wide), 1) + chunk * wide
        spots = stack([
            jnp.where(parent == box - child, 1.0, 0.0).astype(BF16) for child in range(children)
        ])
        spread[:, columns] = dot(high[...], spots) + dot(low[...], spots)
        return 0

    lax.fori_loop(0, chunks, place, 0)

    def finish(chunk, _):
        columns = pl.ds(pl.multiple_of(chunk * wide, wide), wide)
        out[:, columns] = (finished(chunk, fine_ways)[:block] + spread[:, columns]).astype(BF16)
        settle(chunk, fine_ways)
        return 0

    lax.fori_loop(0, chunks, finish, 0)
    settle(0, coarse_ways)
    for copy in up_copies + check_copies + [to_near, coarse_near]:
        copy.wait_send()

    @pl.when(has_other)
    def _():
        to_share.wait_send()
        to_rest.wait_send()
        for copy in spread_copies:
            copy.wait_send()
        coarse_far.wait_send()


def local(spaces, reps, leaf_density, upward_ops, far_ops, downward_ops, fine_lists, coarse_lists):
    rows, boxes = leaf_density.shape
    children, block, _ = upward_ops.shape
    slots = far_ops.shape[0]
    parents = boxes // children
    wide = 256 if boxes % 256 == 0 else boxes
    chunks = boxes // wide
    piece = 128 if boxes >= 256 * reps else boxes // (2 * reps)
    by_row = [ops.transpose(1, 0, 2).reshape(block * children, rows) for ops in (upward_ops, downward_ops)]
    held = -(-block // 16) * 16
    padded = -(-rows // 16) * 16
    vm, dma = pltpu.VMEM, pltpu.SemaphoreType.DMA
    anywhere = pl.BlockSpec(memory_space=pl.ANY)
    inside = pl.BlockSpec(memory_space=vm)
    moving = vm((chunks, reps, held, wide), BF16)
    coarse_moving = vm((1, reps, held, parents), BF16)
    return pl.pallas_call(
        functools.partial(kernel, spaces, reps, wide, piece, block),
        out_shape=jax.ShapeDtypeStruct((block, boxes), BF16),
        in_specs=[anywhere] * 4 + [inside] * 2,
        out_specs=inside,
        scratch_shapes=[
            vm((rows, boxes), BF16), vm((rows, boxes), BF16), vm((rows, boxes), BF16),
            vm((block * children, rows), BF16), vm(far_ops.shape, BF16), vm((block * children, rows), BF16),
            vm(upward_ops.shape, BF16), vm((-(-rows // 128), held * children, 128), F32),
            vm((slots, rows, boxes), BF16), vm((min(256, boxes), wide), BF16),
            moving, moving, moving,
            vm((reps, held, parents), BF16), vm((padded, parents), BF16), vm((padded, 3 * parents), BF16),
            coarse_moving, coarse_moving, coarse_moving,
            vm((reps, held, parents), BF16), vm((rows, parents), F32),
            vm((block, boxes), BF16), vm((block, boxes), BF16), vm((block, boxes), F32),
            dma((4,)), dma((3,)), dma((3,)), dma((reps - 1,)), dma((reps - 1,)), dma((2,)), dma((2,)),
            dma((reps - 1,)), dma((reps - 1,)), dma((reps - 1,)), dma((reps - 1,)),
        ] + [dma((chunks, reps))] * 4 + [dma((1, reps))] * 4,
        compiler_params=pltpu.CompilerParams(
            collective_id=0, has_side_effects=True, vmem_limit_bytes=56 * 2**20),
    )(leaf_density, by_row[0], far_ops, by_row[1], fine_lists, coarse_lists)


def solution(mesh):
    return jax.shard_map(
        functools.partial(local, mesh.shape["space"], mesh.shape["rep"]),
        mesh=mesh,
        in_specs=(
            P(None, "space"),
            P(None, "rep", None),
            P("rep", None, None),
            P(None, "rep", None),
            P("rep", "space"),
            P("rep", "space"),
        ),
        out_specs=P("rep", "space"),
        check_vma=False,
    )
```

```python
import functools

import jax
import jax.numpy as jnp
from jax import lax
from jax.experimental import pallas as pl
from jax.experimental.pallas import tpu as pltpu
from jax.sharding import PartitionSpec as P

coarse_scale = 0.5
F32, BF16 = jnp.float32, jnp.bfloat16
MESH = pl.DeviceIdType.MESH


def dot(a, b):
    return jnp.dot(a, b, preferred_element_type=F32)


def remote(src, dst, send, recv, device):
    return pltpu.make_async_remote_copy(
        src_ref=src, dst_ref=dst, send_sem=send, recv_sem=recv, device_id=device, device_id_type=MESH)


def one_hot(row, count, ramp):
    step = ramp.shape[0]
    pieces = []
    for first in range(0, count, step):
        spot = (row - first).astype(F32).astype(BF16)
        pieces.append(jnp.where(ramp == spot, jnp.ones((), BF16), jnp.zeros((), BF16)))
    return pieces


def stack(pieces):
    return pieces[0] if len(pieces) == 1 else jnp.concatenate(pieces, axis=0)


def blocks_of(total, count, block, held):
    spare = jnp.zeros((held, total.shape[1]), F32)
    total = jnp.concatenate([total, spare], axis=0)
    return [total[j * block:j * block + held] for j in range(count)]


def by_child(tall, children):
    groups, lanes = tall.shape[0] // (children * children), tall.shape[1]
    cube = tall.reshape(groups, children, children, lanes)
    parts = [cube[:, i] for i in range(children)]
    child = lax.broadcasted_iota(jnp.int32, parts[0].shape, 1)
    bit = children // 2
    while bit:
        clear = (child & bit) == 0
        moved = list(parts)
        for i in range(children):
            if i & bit == 0:
                first, second = parts[i], parts[i | bit]
                moved[i] = jnp.where(clear, first, pltpu.roll(second, bit, 1))
                moved[i | bit] = jnp.where(clear, pltpu.roll(first, children - bit, 1), second)
        parts = moved
        bit //= 2
    return [part.reshape(groups * children, lanes) for part in parts]


def kernel(spaces, reps, wide, piece, block,
           density_hbm, up_hbm, far_hbm, down_hbm, lists, coarse_lists, out,
           window, up_raw, far_ops, down_raw, ops, picked, ramp_ref,
           sums, right, left, gathered, coarse_here, coarse_window, coarse_sums, coarse_right, coarse_left,
           checks, full, high, low, spread,
           load_sem, window_send, window_recv, sp_send, sp_recv, cw_send, cw_recv, ag_send, ag_recv, ck_send, ck_recv,
           rs_send, rs_recv, ls_send, ls_recv, crs_send, crs_recv, cls_send, cls_recv):
    s, z = lax.axis_index("space"), lax.axis_index("rep")
    rows, boxes = density_hbm.shape
    density, near, far = (window.at[:, pl.ds(i * boxes, boxes)] for i in range(3))
    slots = far_ops.shape[0]
    children = ops.shape[0]
    parents = boxes // children
    chunks = boxes // wide
    held = sums.shape[2]
    parity = lax.rem(s, 2)
    mate = s + 1 - 2 * parity
    other = s - 1 + 2 * parity
    has_other = jnp.logical_and(other >= 0, other < spaces)

    loads = [
        pltpu.make_async_copy(src, dst, load_sem.at[i])
        for i, (src, dst) in enumerate(
            [(density_hbm, density), (up_hbm, up_raw), (far_hbm, far_ops), (down_hbm, down_raw)])
    ]
    for copy in loads:
        copy.start()

    barrier = pltpu.get_barrier_semaphore()
    for d in range(1, reps):
        pl.semaphore_signal(barrier, inc=1, device_id=(s, lax.rem(z + d, reps)), device_id_type=MESH)
    pl.semaphore_signal(barrier, inc=1, device_id=(mate, z), device_id_type=MESH)

    @pl.when(has_other)
    def _():
        pl.semaphore_signal(barrier, inc=1, device_id=(other, z), device_id_type=MESH)

    ramp_ref[...] = lax.broadcasted_iota(jnp.int32, ramp_ref.shape, 0).astype(F32).astype(BF16)
    pl.semaphore_wait(barrier, reps + has_other.astype(jnp.int32))

    def share(owner):
        return pl.ds(pl.multiple_of(owner * piece, piece), piece)

    rest = pl.ds(reps * piece, boxes - reps * piece)
    to_near = remote(density_hbm, near, window_send.at[0], window_recv.at[0], (mate, z))
    to_share = remote(density_hbm.at[:, share(z)], far.at[:, share(z)],
                      window_send.at[1], window_recv.at[1], (other, z))
    to_rest = remote(density_hbm.at[:, rest], far.at[:, rest], window_send.at[2], window_recv.at[2], (other, z))
    spread_copies = [
        remote(far.at[:, share(z)], far.at[:, share(z)], sp_send.at[d - 1], sp_recv.at[d - 1],
               (s, lax.rem(z + d, reps)))
        for d in range(1, reps)
    ]

    @pl.when(has_other)
    def _():
        to_share.start()
        to_rest.start()

    to_near.start()

    @pl.when(jnp.logical_not(has_other))
    def _():
        far[...] = jnp.zeros((rows, boxes), BF16)
        coarse_window[:, 2 * parents:] = jnp.zeros((coarse_window.shape[0], parents), BF16)

    def put_up():
        lanes = 128 if rows > 128 else rows
        for first in range(0, rows, lanes):
            span = min(lanes, rows - first)
            columns = slice(first, first + span)
            tall = jnp.concatenate(
                [up_raw[:, columns].astype(F32), jnp.zeros((children * (held - block), span), F32)], axis=0)
            if span < lanes:
                tall = jnp.concatenate([tall, jnp.zeros((tall.shape[0], lanes - span), F32)], axis=1)
            for child, value in enumerate(by_child(tall, children)):
                ops[child, :, columns] = value[:block, :span].astype(BF16)

    loads[0].wait()
    loads[1].wait()
    put_up()
    total = jnp.zeros((block, parents), F32)
    for child in range(0, children, 2):
        column = lax.broadcasted_iota(jnp.int32, (1, 2 * parents), 1)
        source = jnp.where(
            column < parents, column * children + child, (column - parents) * children + child + 1)
        pair = dot(density[...], stack(one_hot(source, boxes, ramp_ref[:, :2 * parents]))).astype(BF16)
        total += dot(ops[child], pair[:, :parents])
        total += dot(ops[child + 1], pair[:, parents:])
    gathered[z] = jnp.concatenate([total, jnp.zeros((held - block, parents), F32)], axis=0).astype(BF16)

    def gather_copies(buffer, send, recv):
        return [
            remote(buffer.at[z], buffer.at[z], send.at[d - 1], recv.at[d - 1], (s, lax.rem(z + d, reps)))
            for d in range(1, reps)
        ]

    up_copies = gather_copies(gathered, ag_send, ag_recv)
    for copy in up_copies:
        copy.start()

    @pl.when(has_other)
    def _():
        to_share.wait_recv()
        for copy in spread_copies:
            copy.start()

    def assemble(buffer):
        for j in range(reps):
            full[j * block:(j + 1) * block, :] = buffer[j][:block].astype(F32)
        return full[...].astype(BF16)

    own_base = boxes
    near_base = 2 * boxes * (1 - parity)
    far_base = 2 * boxes * parity
    to_near.wait_recv()

    def pick(chunk, _):
        columns = pl.ds(pl.multiple_of(chunk * wide, wide), wide)
        ramp = ramp_ref[...]
        row = jnp.concatenate([lists[entry:entry + 1, columns] for entry in range(slots)], axis=1)
        spots = one_hot(row - own_base, boxes, ramp) + one_hot(row - near_base, boxes, ramp)
        values = dot(window[:, :2 * boxes], stack(spots))
        for entry in range(slots):
            picked[entry, :, columns] = values[:, entry * wide:(entry + 1) * wide].astype(BF16)
        return 0

    first_part = 1
    lax.fori_loop(0, first_part, pick, 0)

    for copy in up_copies:
        copy.wait_recv()
    coarse_here[...] = jnp.concatenate(
        [assemble(gathered), jnp.zeros((coarse_here.shape[0] - rows, parents), BF16)], axis=0)
    coarse_window[:, :parents] = coarse_here[...]
    coarse_near = remote(
        coarse_here, coarse_window.at[:, pl.ds(parents, parents)], cw_send.at[0], cw_recv.at[0], (mate, z))
    coarse_far = remote(
        coarse_here, coarse_window.at[:, pl.ds(2 * parents, parents)], cw_send.at[1], cw_recv.at[1], (other, z))
    coarse_near.start()

    @pl.when(has_other)
    def _():
        coarse_far.start()

    lax.fori_loop(first_part, chunks, pick, 0)

    loads[2].wait()
    coarse_near.wait_recv()

    @pl.when(has_other)
    def _():
        coarse_far.wait_recv()

    total = jnp.zeros((rows, parents), F32)
    row = jnp.concatenate([coarse_lists[entry:entry + 1, :] for entry in range(slots)], axis=1)
    ramp = lax.broadcasted_iota(jnp.int32, (parents, slots * parents), 0)
    place = [
        jnp.where(ramp == row - base, 1.0, 0.0).astype(BF16)
        for base in (own_base // children, near_base // children, far_base // children)
    ]
    values = dot(coarse_window[:rows, :], stack(place)).astype(BF16)
    for entry in range(slots):
        total += dot(far_ops[entry], values[:, entry * parents:(entry + 1) * parents])
    for j, value in enumerate(blocks_of(coarse_scale * total, reps, block, held)):
        coarse_sums[0, j] = value.astype(BF16)

    def move_right(chunk, ways, j):
        _, buffer, _, send, recv, _, _ = ways
        return remote(buffer.at[chunk, j], buffer.at[chunk, j], send.at[chunk, j], recv.at[chunk, j], (s, z + 1))

    def move_left(chunk, ways, j):
        _, _, buffer, _, _, send, recv = ways
        return remote(buffer.at[chunk, j], buffer.at[chunk, j], send.at[chunk, j], recv.at[chunk, j], (s, z - 1))

    def forward_right(chunk, ways):
        mine, buffer = ways[0], ways[1]
        for j in reversed(range(1, reps)):
            @pl.when(j > z)
            def _(j=j):
                copy = move_right(chunk, ways, j)

                @pl.when(z > 0)
                def _():
                    copy.wait_recv()
                    buffer[chunk, j] = (buffer[chunk, j].astype(F32) + mine[chunk, j].astype(F32)).astype(BF16)

                @pl.when(z == 0)
                def _():
                    buffer[chunk, j] = mine[chunk, j]

                copy.start()

    def forward_left(chunk, ways):
        mine, buffer = ways[0], ways[2]
        for j in range(reps - 1):
            @pl.when(j < z)
            def _(j=j):
                copy = move_left(chunk, ways, j)

                @pl.when(z < reps - 1)
                def _():
                    copy.wait_recv()
                    buffer[chunk, j] = (buffer[chunk, j].astype(F32) + mine[chunk, j].astype(F32)).astype(BF16)

                @pl.when(z == reps - 1)
                def _():
                    buffer[chunk, j] = mine[chunk, j]

                copy.start()

    def finished(chunk, ways):
        mine, go_right, go_left = ways[:3]

        @pl.when(z > 0)
        def _():
            move_right(chunk, ways, z).wait_recv()

        @pl.when(z == 0)
        def _():
            go_right[chunk, z] = jnp.zeros(go_right.shape[2:], BF16)

        @pl.when(z < reps - 1)
        def _():
            move_left(chunk, ways, z).wait_recv()

        @pl.when(z == reps - 1)
        def _():
            go_left[chunk, z] = jnp.zeros(go_left.shape[2:], BF16)

        return mine[chunk, z].astype(F32) + go_right[chunk, z].astype(F32) + go_left[chunk, z].astype(F32)

    def settle(chunk, ways):
        for j in range(reps):
            @pl.when(j > z)
            def _(j=j):
                move_right(chunk, ways, j).wait_send()

            @pl.when(j < z)
            def _(j=j):
                move_left(chunk, ways, j).wait_send()

    fine_ways = (sums, right, left, rs_send, rs_recv, ls_send, ls_recv)
    coarse_ways = (coarse_sums, coarse_right, coarse_left, crs_send, crs_recv, cls_send, cls_recv)

    def coarse_step(t):
        @pl.when(t == z)
        def _():
            forward_right(0, coarse_ways)

        @pl.when(t == reps - 1 - z)
        def _():
            forward_left(0, coarse_ways)

    def step(t):
        coarse_step(t + 1)

        @pl.when(jnp.logical_and(t >= z, t - z < chunks))
        def _():
            forward_right(t - z, fine_ways)

        back = reps - 1 - z

        @pl.when(jnp.logical_and(t >= back, t - back < chunks))
        def _():
            forward_left(t - back, fine_ways)

    def translate(t, _):
        columns = pl.ds(pl.multiple_of(t * wide, wide), wide)
        ramp = ramp_ref[...]
        total = jnp.zeros((rows, wide), F32)
        row = jnp.concatenate([lists[entry:entry + 1, columns] for entry in range(slots)], axis=1)
        values = dot(window[:, 2 * boxes:], stack(one_hot(row - far_base, boxes, ramp)))
        for entry in range(slots):
            source = values[:, entry * wide:(entry + 1) * wide] + picked[entry, :, columns].astype(F32)
            total += dot(far_ops[entry], source.astype(BF16))
        for j, value in enumerate(blocks_of(total, reps, block, held)):
            sums[t, j] = value.astype(BF16)
        step(t)
        return 0

    coarse_step(0)

    @pl.when(has_other)
    def _():
        to_rest.wait_recv()
        for copy in spread_copies:
            copy.wait_recv()

    lax.fori_loop(0, chunks, translate, 0)

    check_copies = gather_copies(checks, ck_send, ck_recv)
    for t in range(chunks, chunks + reps - 1):
        step(t)
        if t == max(chunks, reps - 1):
            checks[z] = finished(0, coarse_ways).astype(BF16)
            for copy in check_copies:
                copy.start()

    for copy in check_copies:
        copy.wait_recv()
    check = assemble(checks)
    loads[3].wait()
    term = jnp.concatenate(
        [dot(down_raw[...], check), jnp.zeros((children * (held - block), parents), F32)], axis=0)
    for child, value in enumerate(by_child(term, children)):
        top = value[:block].astype(BF16)
        columns = pl.ds(child * parents, parents)
        high[:, columns] = top
        low[:, columns] = (value[:block] - top.astype(F32)).astype(BF16)

    def place(chunk, _):
        columns = pl.ds(pl.multiple_of(chunk * wide, wide), wide)
        parent = lax.broadcasted_iota(jnp.int32, (parents, wide), 0) * children
        box = lax.broadcasted_iota(jnp.int32, (parents, wide), 1) + chunk * wide
        spots = stack([
            jnp.where(parent == box - child, 1.0, 0.0).astype(BF16) for child in range(children)
        ])
        spread[:, columns] = dot(high[...], spots) + dot(low[...], spots)
        return 0

    lax.fori_loop(0, chunks, place, 0)

    def finish(chunk, _):
        columns = pl.ds(pl.multiple_of(chunk * wide, wide), wide)
        out[:, columns] = (finished(chunk, fine_ways)[:block] + spread[:, columns]).astype(BF16)
        settle(chunk, fine_ways)
        return 0

    lax.fori_loop(0, chunks, finish, 0)
    settle(0, coarse_ways)
    for copy in up_copies + check_copies + [to_near, coarse_near]:
        copy.wait_send()

    @pl.when(has_other)
    def _():
        to_share.wait_send()
        to_rest.wait_send()
        for copy in spread_copies:
            copy.wait_send()
        coarse_far.wait_send()


def local(spaces, reps, leaf_density, upward_ops, far_ops, downward_ops, fine_lists, coarse_lists):
    rows, boxes = leaf_density.shape
    children, block, _ = upward_ops.shape
    slots = far_ops.shape[0]
    parents = boxes // children
    wide = 256 if boxes % 256 == 0 else boxes
    chunks = boxes // wide
    piece = 128 if boxes >= 256 * reps else boxes // (2 * reps)
    by_row = [ops.transpose(1, 0, 2).reshape(block * children, rows) for ops in (upward_ops, downward_ops)]
    held = -(-block // 16) * 16
    padded = -(-rows // 16) * 16
    vm, dma = pltpu.VMEM, pltpu.SemaphoreType.DMA
    anywhere = pl.BlockSpec(memory_space=pl.ANY)
    inside = pl.BlockSpec(memory_space=vm)
    moving = vm((chunks, reps, held, wide), BF16)
    coarse_moving = vm((1, reps, held, parents), BF16)
    return pl.pallas_call(
        functools.partial(kernel, spaces, reps, wide, piece, block),
        out_shape=jax.ShapeDtypeStruct((block, boxes), BF16),
        in_specs=[anywhere] * 4 + [inside] * 2,
        out_specs=inside,
        scratch_shapes=[
            vm((rows, 3 * boxes), BF16),
            vm((block * children, rows), BF16), vm(far_ops.shape, BF16), vm((block * children, rows), BF16),
            vm(upward_ops.shape, BF16),
            vm((slots, rows, boxes), BF16), vm((min(256, boxes), slots * wide), BF16),
            moving, moving, moving,
            vm((reps, held, parents), BF16), vm((padded, parents), BF16), vm((padded, 3 * parents), BF16),
            coarse_moving, coarse_moving, coarse_moving,
            vm((reps, held, parents), BF16), vm((rows, parents), F32),
            vm((block, boxes), BF16), vm((block, boxes), BF16), vm((block, boxes), F32),
            dma((4,)), dma((3,)), dma((3,)), dma((reps - 1,)), dma((reps - 1,)), dma((2,)), dma((2,)),
            dma((reps - 1,)), dma((reps - 1,)), dma((reps - 1,)), dma((reps - 1,)),
        ] + [dma((chunks, reps))] * 4 + [dma((1, reps))] * 4,
        compiler_params=pltpu.CompilerParams(
            collective_id=0, has_side_effects=True, vmem_limit_bytes=56 * 2**20),
    )(leaf_density, by_row[0], far_ops, by_row[1], fine_lists, coarse_lists)


def solution(mesh):
    return jax.shard_map(
        functools.partial(local, mesh.shape["space"], mesh.shape["rep"]),
        mesh=mesh,
        in_specs=(
            P(None, "space"),
            P(None, "rep", None),
            P("rep", None, None),
            P(None, "rep", None),
            P("rep", "space"),
            P("rep", "space"),
        ),
        out_specs=P("rep", "space"),
        check_vma=False,
    )
```

```python
import functools

import jax
import jax.numpy as jnp
from jax import lax
from jax.experimental import pallas as pl
from jax.experimental.pallas import tpu as pltpu
from jax.sharding import PartitionSpec as P

coarse_scale = 0.5
F32, BF16 = jnp.float32, jnp.bfloat16
MESH = pl.DeviceIdType.MESH


def dot(a, b):
    return jnp.dot(a, b, preferred_element_type=F32)


def remote(src, dst, send, recv, device):
    return pltpu.make_async_remote_copy(
        src_ref=src, dst_ref=dst, send_sem=send, recv_sem=recv, device_id=device, device_id_type=MESH)


def one_hot(row, count, ramp):
    step = ramp.shape[0]
    pieces = []
    for first in range(0, count, step):
        spot = (row - first).astype(F32).astype(BF16)
        pieces.append(jnp.where(ramp == spot, jnp.ones((), BF16), jnp.zeros((), BF16)))
    return pieces


def stack(pieces):
    return pieces[0] if len(pieces) == 1 else jnp.concatenate(pieces, axis=0)


def blocks_of(total, count, block, held):
    spare = jnp.zeros((held, total.shape[1]), F32)
    total = jnp.concatenate([total, spare], axis=0)
    return [total[j * block:j * block + held] for j in range(count)]


def by_child(tall, children):
    groups, lanes = tall.shape[0] // (children * children), tall.shape[1]
    cube = tall.reshape(groups, children, children, lanes)
    parts = [cube[:, i] for i in range(children)]
    child = lax.broadcasted_iota(jnp.int32, parts[0].shape, 1)
    bit = children // 2
    while bit:
        clear = (child & bit) == 0
        moved = list(parts)
        for i in range(children):
            if i & bit == 0:
                first, second = parts[i], parts[i | bit]
                moved[i] = jnp.where(clear, first, pltpu.roll(second, bit, 1))
                moved[i | bit] = jnp.where(clear, pltpu.roll(first, children - bit, 1), second)
        parts = moved
        bit //= 2
    return [part.reshape(groups * children, lanes) for part in parts]


def kernel(spaces, reps, wide, piece, block,
           density_hbm, up_hbm, far_hbm, down_hbm, lists, coarse_lists, out,
           window, up_raw, far_ops, down_raw, ops, picked, ramp_ref,
           sums, right, left, gathered, coarse_here, coarse_window, coarse_sums, coarse_right, coarse_left,
           checks, full, high, low, spread,
           load_sem, window_send, window_recv, sp_send, sp_recv, cw_send, cw_recv, ag_send, ag_recv, ck_send, ck_recv,
           rs_send, rs_recv, ls_send, ls_recv, crs_send, crs_recv, cls_send, cls_recv):
    s, z = lax.axis_index("space"), lax.axis_index("rep")
    rows, boxes = density_hbm.shape
    density, near, far = (window.at[:, pl.ds(i * boxes, boxes)] for i in range(3))
    slots = far_ops.shape[0]
    children = ops.shape[0]
    parents = boxes // children
    chunks = boxes // wide
    held = sums.shape[2]
    parity = lax.rem(s, 2)
    mate = s + 1 - 2 * parity
    other = s - 1 + 2 * parity
    has_other = jnp.logical_and(other >= 0, other < spaces)

    loads = [
        pltpu.make_async_copy(src, dst, load_sem.at[i])
        for i, (src, dst) in enumerate(
            [(density_hbm, density), (up_hbm, up_raw), (far_hbm, far_ops), (down_hbm, down_raw)])
    ]
    for copy in loads:
        copy.start()

    barrier = pltpu.get_barrier_semaphore()
    for d in range(1, reps):
        pl.semaphore_signal(barrier, inc=1, device_id=(s, lax.rem(z + d, reps)), device_id_type=MESH)
    pl.semaphore_signal(barrier, inc=1, device_id=(mate, z), device_id_type=MESH)

    @pl.when(has_other)
    def _():
        pl.semaphore_signal(barrier, inc=1, device_id=(other, z), device_id_type=MESH)

    ramp_ref[...] = lax.broadcasted_iota(jnp.int32, ramp_ref.shape, 0).astype(F32).astype(BF16)
    pl.semaphore_wait(barrier, reps + has_other.astype(jnp.int32))

    def share(owner):
        return pl.ds(pl.multiple_of(owner * piece, piece), piece)

    def is_helped(target):
        return jnp.logical_and(lax.rem(target, 8) != 2, lax.rem(target, 8) != 5)

    helped = jnp.logical_and(has_other, is_helped(s))
    helps = jnp.logical_and(has_other, is_helped(other))
    whole_in = jnp.logical_and(has_other, jnp.logical_not(is_helped(s)))
    whole_out = jnp.logical_and(has_other, jnp.logical_not(is_helped(other)))
    first = pl.ds(0, reps * piece)
    rest = pl.ds(reps * piece, boxes - reps * piece)
    to_first = remote(density_hbm.at[:, first], far.at[:, first], window_send.at[3], window_recv.at[3], (other, z))
    to_near = remote(density_hbm, near, window_send.at[0], window_recv.at[0], (mate, z))
    to_share = remote(density_hbm.at[:, share(z)], far.at[:, share(z)],
                      window_send.at[1], window_recv.at[1], (other, z))
    to_rest = remote(density_hbm.at[:, rest], far.at[:, rest], window_send.at[2], window_recv.at[2], (other, z))
    spread_copies = [
        remote(far.at[:, share(z)], far.at[:, share(z)], sp_send.at[d - 1], sp_recv.at[d - 1],
               (s, lax.rem(z + d, reps)))
        for d in range(1, reps)
    ]

    @pl.when(helps)
    def _():
        to_share.start()

    @pl.when(whole_out)
    def _():
        to_first.start()

    to_near.start()

    @pl.when(jnp.logical_not(has_other))
    def _():
        far[...] = jnp.zeros((rows, boxes), BF16)
        coarse_window[:, 2 * parents:] = jnp.zeros((coarse_window.shape[0], parents), BF16)

    def put_up():
        lanes = 128 if rows > 128 else rows
        for first in range(0, rows, lanes):
            span = min(lanes, rows - first)
            columns = slice(first, first + span)
            tall = jnp.concatenate(
                [up_raw[:, columns].astype(F32), jnp.zeros((children * (held - block), span), F32)], axis=0)
            if span < lanes:
                tall = jnp.concatenate([tall, jnp.zeros((tall.shape[0], lanes - span), F32)], axis=1)
            for child, value in enumerate(by_child(tall, children)):
                ops[child, :, columns] = value[:block, :span].astype(BF16)

    loads[0].wait()
    loads[1].wait()
    put_up()
    total = jnp.zeros((block, parents), F32)
    for child in range(0, children, 2):
        column = lax.broadcasted_iota(jnp.int32, (1, 2 * parents), 1)
        source = jnp.where(
            column < parents, column * children + child, (column - parents) * children + child + 1)
        pair = dot(density[...], stack(one_hot(source, boxes, ramp_ref[:, :2 * parents]))).astype(BF16)
        total += dot(ops[child], pair[:, :parents])
        total += dot(ops[child + 1], pair[:, parents:])
    gathered[z] = jnp.concatenate([total, jnp.zeros((held - block, parents), F32)], axis=0).astype(BF16)

    def gather_copies(buffer, send, recv):
        return [
            remote(buffer.at[z], buffer.at[z], send.at[d - 1], recv.at[d - 1], (s, lax.rem(z + d, reps)))
            for d in range(1, reps)
        ]

    up_copies = gather_copies(gathered, ag_send, ag_recv)
    for copy in up_copies:
        copy.start()

    @pl.when(has_other)
    def _():
        to_rest.start()

    @pl.when(helped)
    def _():
        to_share.wait_recv()
        for copy in spread_copies:
            copy.start()

    def assemble(buffer):
        for j in range(reps):
            full[j * block:(j + 1) * block, :] = buffer[j][:block].astype(F32)
        return full[...].astype(BF16)

    own_base = boxes
    near_base = 2 * boxes * (1 - parity)
    far_base = 2 * boxes * parity
    head = reps * piece
    to_near.wait_recv()

    def pick(chunk, _):
        columns = pl.ds(pl.multiple_of(chunk * wide, wide), wide)
        ramp = ramp_ref[...]
        row = jnp.concatenate([lists[entry:entry + 1, columns] for entry in range(slots)], axis=1)
        spots = one_hot(row - own_base, boxes, ramp) + one_hot(row - near_base, boxes, ramp)
        values = dot(window[:, :2 * boxes], stack(spots))
        for entry in range(slots):
            picked[entry, :, columns] = values[:, entry * wide:(entry + 1) * wide].astype(BF16)
        return 0

    first_part = 1
    lax.fori_loop(0, first_part, pick, 0)

    for copy in up_copies:
        copy.wait_recv()
    coarse_here[...] = jnp.concatenate(
        [assemble(gathered), jnp.zeros((coarse_here.shape[0] - rows, parents), BF16)], axis=0)
    coarse_window[:, :parents] = coarse_here[...]
    coarse_near = remote(
        coarse_here, coarse_window.at[:, pl.ds(parents, parents)], cw_send.at[0], cw_recv.at[0], (mate, z))
    coarse_far = remote(
        coarse_here, coarse_window.at[:, pl.ds(2 * parents, parents)], cw_send.at[1], cw_recv.at[1], (other, z))
    coarse_near.start()

    @pl.when(has_other)
    def _():
        coarse_far.start()

    lax.fori_loop(first_part, chunks, pick, 0)

    loads[2].wait()
    coarse_near.wait_recv()

    @pl.when(has_other)
    def _():
        coarse_far.wait_recv()

    total = jnp.zeros((rows, parents), F32)
    row = jnp.concatenate([coarse_lists[entry:entry + 1, :] for entry in range(slots)], axis=1)
    ramp = lax.broadcasted_iota(jnp.int32, (parents, slots * parents), 0)
    place = [
        jnp.where(ramp == row - base, 1.0, 0.0).astype(BF16)
        for base in (own_base // children, near_base // children, far_base // children)
    ]
    values = dot(coarse_window[:rows, :], stack(place)).astype(BF16)
    for entry in range(slots):
        total += dot(far_ops[entry], values[:, entry * parents:(entry + 1) * parents])
    for j, value in enumerate(blocks_of(coarse_scale * total, reps, block, held)):
        coarse_sums[0, j] = value.astype(BF16)

    def move_right(chunk, ways, j):
        _, buffer, _, send, recv, _, _ = ways
        return remote(buffer.at[chunk, j], buffer.at[chunk, j], send.at[chunk, j], recv.at[chunk, j], (s, z + 1))

    def move_left(chunk, ways, j):
        _, _, buffer, _, _, send, recv = ways
        return remote(buffer.at[chunk, j], buffer.at[chunk, j], send.at[chunk, j], recv.at[chunk, j], (s, z - 1))

    def forward_right(chunk, ways):
        mine, buffer = ways[0], ways[1]
        for j in reversed(range(1, reps)):
            @pl.when(j > z)
            def _(j=j):
                copy = move_right(chunk, ways, j)

                @pl.when(z > 0)
                def _():
                    copy.wait_recv()
                    buffer[chunk, j] = (buffer[chunk, j].astype(F32) + mine[chunk, j].astype(F32)).astype(BF16)

                @pl.when(z == 0)
                def _():
                    buffer[chunk, j] = mine[chunk, j]

                copy.start()

    def forward_left(chunk, ways):
        mine, buffer = ways[0], ways[2]
        for j in range(reps - 1):
            @pl.when(j < z)
            def _(j=j):
                copy = move_left(chunk, ways, j)

                @pl.when(z < reps - 1)
                def _():
                    copy.wait_recv()
                    buffer[chunk, j] = (buffer[chunk, j].astype(F32) + mine[chunk, j].astype(F32)).astype(BF16)

                @pl.when(z == reps - 1)
                def _():
                    buffer[chunk, j] = mine[chunk, j]

                copy.start()

    def finished(chunk, ways):
        mine, go_right, go_left = ways[:3]

        @pl.when(z > 0)
        def _():
            move_right(chunk, ways, z).wait_recv()

        @pl.when(z == 0)
        def _():
            go_right[chunk, z] = jnp.zeros(go_right.shape[2:], BF16)

        @pl.when(z < reps - 1)
        def _():
            move_left(chunk, ways, z).wait_recv()

        @pl.when(z == reps - 1)
        def _():
            go_left[chunk, z] = jnp.zeros(go_left.shape[2:], BF16)

        return mine[chunk, z].astype(F32) + go_right[chunk, z].astype(F32) + go_left[chunk, z].astype(F32)

    def settle(chunk, ways):
        for j in range(reps):
            @pl.when(j > z)
            def _(j=j):
                move_right(chunk, ways, j).wait_send()

            @pl.when(j < z)
            def _(j=j):
                move_left(chunk, ways, j).wait_send()

    fine_ways = (sums, right, left, rs_send, rs_recv, ls_send, ls_recv)
    coarse_ways = (coarse_sums, coarse_right, coarse_left, crs_send, crs_recv, cls_send, cls_recv)

    def coarse_step(t):
        @pl.when(t == z)
        def _():
            forward_right(0, coarse_ways)

        @pl.when(t == reps - 1 - z)
        def _():
            forward_left(0, coarse_ways)

    def step(t):
        coarse_step(t + 1)

        @pl.when(jnp.logical_and(t >= z, t - z < chunks))
        def _():
            forward_right(t - z, fine_ways)

        back = reps - 1 - z

        @pl.when(jnp.logical_and(t >= back, t - back < chunks))
        def _():
            forward_left(t - back, fine_ways)

    def translate(t, _):
        columns = pl.ds(pl.multiple_of(t * wide, wide), wide)
        ramp = ramp_ref[...]
        total = jnp.zeros((rows, wide), F32)
        row = jnp.concatenate([lists[entry:entry + 1, columns] for entry in range(slots)], axis=1)
        values = dot(window[:, 2 * boxes + head:], stack(one_hot(row - far_base - head, boxes - head, ramp)))
        for entry in range(slots):
            source = values[:, entry * wide:(entry + 1) * wide] + picked[entry, :, columns].astype(F32)
            total += dot(far_ops[entry], source.astype(BF16))
        for j, value in enumerate(blocks_of(total, reps, block, held)):
            sums[t, j] = value.astype(BF16)
        step(t)
        return 0

    coarse_step(0)

    @pl.when(helped)
    def _():
        for copy in spread_copies:
            copy.wait_recv()

    @pl.when(whole_in)
    def _():
        to_first.wait_recv()

    def pick_first(chunk, _):
        columns = pl.ds(pl.multiple_of(chunk * wide, wide), wide)
        row = jnp.concatenate([lists[entry:entry + 1, columns] for entry in range(slots)], axis=1)
        values = dot(window[:, 2 * boxes:2 * boxes + head], stack(one_hot(row - far_base, head, ramp_ref[...])))
        for entry in range(slots):
            part = values[:, entry * wide:(entry + 1) * wide] + picked[entry, :, columns].astype(F32)
            picked[entry, :, columns] = part.astype(BF16)
        return 0

    lax.fori_loop(0, chunks, pick_first, 0)

    @pl.when(has_other)
    def _():
        to_rest.wait_recv()

    lax.fori_loop(0, chunks, translate, 0)

    check_copies = gather_copies(checks, ck_send, ck_recv)
    for t in range(chunks, chunks + reps - 1):
        step(t)
        if t == max(chunks, reps - 1):
            checks[z] = finished(0, coarse_ways).astype(BF16)
            for copy in check_copies:
                copy.start()

    for copy in check_copies:
        copy.wait_recv()
    check = assemble(checks)
    loads[3].wait()
    term = jnp.concatenate(
        [dot(down_raw[...], check), jnp.zeros((children * (held - block), parents), F32)], axis=0)
    for child, value in enumerate(by_child(term, children)):
        top = value[:block].astype(BF16)
        columns = pl.ds(child * parents, parents)
        high[:, columns] = top
        low[:, columns] = (value[:block] - top.astype(F32)).astype(BF16)

    def place(chunk, _):
        columns = pl.ds(pl.multiple_of(chunk * wide, wide), wide)
        parent = lax.broadcasted_iota(jnp.int32, (parents, wide), 0) * children
        box = lax.broadcasted_iota(jnp.int32, (parents, wide), 1) + chunk * wide
        spots = stack([
            jnp.where(parent == box - child, 1.0, 0.0).astype(BF16) for child in range(children)
        ])
        spread[:, columns] = dot(high[...], spots) + dot(low[...], spots)
        return 0

    lax.fori_loop(0, chunks, place, 0)

    def finish(chunk, _):
        columns = pl.ds(pl.multiple_of(chunk * wide, wide), wide)
        out[:, columns] = (finished(chunk, fine_ways)[:block] + spread[:, columns]).astype(BF16)
        settle(chunk, fine_ways)
        return 0

    lax.fori_loop(0, chunks, finish, 0)
    settle(0, coarse_ways)
    for copy in up_copies + check_copies + [to_near, coarse_near]:
        copy.wait_send()

    @pl.when(has_other)
    def _():
        to_rest.wait_send()

    @pl.when(helps)
    def _():
        to_share.wait_send()

    @pl.when(whole_out)
    def _():
        to_first.wait_send()

    @pl.when(helped)
    def _():
        for copy in spread_copies:
            copy.wait_send()

    @pl.when(has_other)
    def _():
        coarse_far.wait_send()


def local(spaces, reps, leaf_density, upward_ops, far_ops, downward_ops, fine_lists, coarse_lists):
    rows, boxes = leaf_density.shape
    children, block, _ = upward_ops.shape
    slots = far_ops.shape[0]
    parents = boxes // children
    wide = 256 if boxes % 256 == 0 else boxes
    chunks = boxes // wide
    piece = 128 if boxes >= 256 * reps else boxes // (2 * reps)
    by_row = [ops.transpose(1, 0, 2).reshape(block * children, rows) for ops in (upward_ops, downward_ops)]
    held = -(-block // 16) * 16
    padded = -(-rows // 16) * 16
    vm, dma = pltpu.VMEM, pltpu.SemaphoreType.DMA
    anywhere = pl.BlockSpec(memory_space=pl.ANY)
    inside = pl.BlockSpec(memory_space=vm)
    moving = vm((chunks, reps, held, wide), BF16)
    coarse_moving = vm((1, reps, held, parents), BF16)
    return pl.pallas_call(
        functools.partial(kernel, spaces, reps, wide, piece, block),
        out_shape=jax.ShapeDtypeStruct((block, boxes), BF16),
        in_specs=[anywhere] * 4 + [inside] * 2,
        out_specs=inside,
        scratch_shapes=[
            vm((rows, 3 * boxes), BF16),
            vm((block * children, rows), BF16), vm(far_ops.shape, BF16), vm((block * children, rows), BF16),
            vm(upward_ops.shape, BF16),
            vm((slots, rows, boxes), BF16), vm((min(256, boxes), slots * wide), BF16),
            moving, moving, moving,
            vm((reps, held, parents), BF16), vm((padded, parents), BF16), vm((padded, 3 * parents), BF16),
            coarse_moving, coarse_moving, coarse_moving,
            vm((reps, held, parents), BF16), vm((rows, parents), F32),
            vm((block, boxes), BF16), vm((block, boxes), BF16), vm((block, boxes), F32),
            dma((4,)), dma((4,)), dma((4,)), dma((reps - 1,)), dma((reps - 1,)), dma((2,)), dma((2,)),
            dma((reps - 1,)), dma((reps - 1,)), dma((reps - 1,)), dma((reps - 1,)),
        ] + [dma((chunks, reps))] * 4 + [dma((1, reps))] * 4,
        compiler_params=pltpu.CompilerParams(
            collective_id=0, has_side_effects=True, vmem_limit_bytes=56 * 2**20),
    )(leaf_density, by_row[0], far_ops, by_row[1], fine_lists, coarse_lists)


def solution(mesh):
    return jax.shard_map(
        functools.partial(local, mesh.shape["space"], mesh.shape["rep"]),
        mesh=mesh,
        in_specs=(
            P(None, "space"),
            P(None, "rep", None),
            P("rep", None, None),
            P(None, "rep", None),
            P("rep", "space"),
            P("rep", "space"),
        ),
        out_specs=P("rep", "space"),
        check_vma=False,
    )
```

```python
import functools

import jax
import jax.numpy as jnp
from jax import lax
from jax.experimental import pallas as pl
from jax.experimental.pallas import tpu as pltpu
from jax.sharding import PartitionSpec as P

coarse_scale = 0.5
F32, BF16 = jnp.float32, jnp.bfloat16
MESH = pl.DeviceIdType.MESH


def dot(a, b):
    return jnp.dot(a, b, preferred_element_type=F32)


def remote(src, dst, send, recv, device):
    return pltpu.make_async_remote_copy(
        src_ref=src, dst_ref=dst, send_sem=send, recv_sem=recv, device_id=device, device_id_type=MESH)


def one_hot(row, count, ramp):
    step = ramp.shape[0]
    pieces = []
    for first in range(0, count, step):
        spot = (row - first).astype(F32).astype(BF16)
        pieces.append(jnp.where(ramp == spot, jnp.ones((), BF16), jnp.zeros((), BF16)))
    return pieces


def stack(pieces):
    return pieces[0] if len(pieces) == 1 else jnp.concatenate(pieces, axis=0)


def blocks_of(total, count, block, held):
    spare = jnp.zeros((held, total.shape[1]), F32)
    total = jnp.concatenate([total, spare], axis=0)
    return [total[j * block:j * block + held] for j in range(count)]


def by_child(tall, children):
    groups, lanes = tall.shape[0] // (children * children), tall.shape[1]
    cube = tall.reshape(groups, children, children, lanes)
    parts = [cube[:, i] for i in range(children)]
    child = lax.broadcasted_iota(jnp.int32, parts[0].shape, 1)
    bit = children // 2
    while bit:
        clear = (child & bit) == 0
        moved = list(parts)
        for i in range(children):
            if i & bit == 0:
                first, second = parts[i], parts[i | bit]
                moved[i] = jnp.where(clear, first, pltpu.roll(second, bit, 1))
                moved[i | bit] = jnp.where(clear, pltpu.roll(first, children - bit, 1), second)
        parts = moved
        bit //= 2
    return [part.reshape(groups * children, lanes) for part in parts]


def kernel(spaces, reps, wide, piece, block,
           density_hbm, up_hbm, far_hbm, down_hbm, lists, coarse_lists, out,
           window, up_raw, far_ops, down_raw, ops, picked, ramp_ref,
           sums, right, left, gathered, coarse_here, coarse_window, coarse_sums, coarse_right, coarse_left,
           checks, full, high, low, spread,
           load_sem, window_send, window_recv, sp_send, sp_recv, cw_send, cw_recv, ag_send, ag_recv, ck_send, ck_recv,
           rs_send, rs_recv, ls_send, ls_recv, crs_send, crs_recv, cls_send, cls_recv):
    s, z = lax.axis_index("space"), lax.axis_index("rep")
    rows, boxes = density_hbm.shape
    density, near, far = (window.at[:, pl.ds(i * boxes, boxes)] for i in range(3))
    slots = far_ops.shape[0]
    children = ops.shape[0]
    parents = boxes // children
    chunks = boxes // wide
    held = sums.shape[2]
    parity = lax.rem(s, 2)
    mate = s + 1 - 2 * parity
    other = s - 1 + 2 * parity
    has_other = jnp.logical_and(other >= 0, other < spaces)

    loads = [
        pltpu.make_async_copy(src, dst, load_sem.at[i])
        for i, (src, dst) in enumerate(
            [(density_hbm, density), (up_hbm, up_raw), (far_hbm, far_ops), (down_hbm, down_raw)])
    ]
    for copy in loads:
        copy.start()

    barrier = pltpu.get_barrier_semaphore()
    for d in range(1, reps):
        pl.semaphore_signal(barrier, inc=1, device_id=(s, lax.rem(z + d, reps)), device_id_type=MESH)
    pl.semaphore_signal(barrier, inc=1, device_id=(mate, z), device_id_type=MESH)

    @pl.when(has_other)
    def _():
        pl.semaphore_signal(barrier, inc=1, device_id=(other, z), device_id_type=MESH)

    ramp_ref[...] = lax.broadcasted_iota(jnp.int32, ramp_ref.shape, 0).astype(F32).astype(BF16)
    pl.semaphore_wait(barrier, reps + has_other.astype(jnp.int32))

    def share(owner):
        return pl.ds(pl.multiple_of(owner * piece, piece), piece)

    def is_helped(target):
        return jnp.logical_and(lax.rem(target, 8) != 2, lax.rem(target, 8) != 5)

    helped = jnp.logical_and(has_other, is_helped(s))
    helps = jnp.logical_and(has_other, is_helped(other))
    whole_in = jnp.logical_and(has_other, jnp.logical_not(is_helped(s)))
    whole_out = jnp.logical_and(has_other, jnp.logical_not(is_helped(other)))
    first = pl.ds(0, reps * piece)
    rest = pl.ds(reps * piece, boxes - reps * piece)
    to_first = remote(density_hbm.at[:, first], far.at[:, first], window_send.at[3], window_recv.at[3], (other, z))
    to_near = remote(density_hbm, near, window_send.at[0], window_recv.at[0], (mate, z))
    to_share = remote(density_hbm.at[:, share(z)], far.at[:, share(z)],
                      window_send.at[1], window_recv.at[1], (other, z))
    to_rest = remote(density_hbm.at[:, rest], far.at[:, rest], window_send.at[2], window_recv.at[2], (other, z))
    spread_copies = [
        remote(far.at[:, share(z)], far.at[:, share(z)], sp_send.at[d - 1], sp_recv.at[d - 1],
               (s, lax.rem(z + d, reps)))
        for d in range(1, reps)
    ]

    @pl.when(helps)
    def _():
        to_share.start()

    @pl.when(whole_out)
    def _():
        to_first.start()

    to_near.start()

    @pl.when(jnp.logical_not(has_other))
    def _():
        far[...] = jnp.zeros((rows, boxes), BF16)
        coarse_window[:, 2 * parents:] = jnp.zeros((coarse_window.shape[0], parents), BF16)

    def put_up():
        lanes = 128 if rows > 128 else rows
        for first in range(0, rows, lanes):
            span = min(lanes, rows - first)
            columns = slice(first, first + span)
            tall = jnp.concatenate(
                [up_raw[:, columns].astype(F32), jnp.zeros((children * (held - block), span), F32)], axis=0)
            if span < lanes:
                tall = jnp.concatenate([tall, jnp.zeros((tall.shape[0], lanes - span), F32)], axis=1)
            for child, value in enumerate(by_child(tall, children)):
                ops[child, :, columns] = value[:block, :span].astype(BF16)

    loads[0].wait()
    loads[1].wait()
    put_up()
    total = jnp.zeros((block, parents), F32)
    for child in range(0, children, 2):
        column = lax.broadcasted_iota(jnp.int32, (1, 2 * parents), 1)
        source = jnp.where(
            column < parents, column * children + child, (column - parents) * children + child + 1)
        pair = dot(density[...], stack(one_hot(source, boxes, ramp_ref[:, :2 * parents]))).astype(BF16)
        total += dot(ops[child], pair[:, :parents])
        total += dot(ops[child + 1], pair[:, parents:])
    gathered[z] = jnp.concatenate([total, jnp.zeros((held - block, parents), F32)], axis=0).astype(BF16)

    def gather_copies(buffer, send, recv):
        return [
            remote(buffer.at[z], buffer.at[z], send.at[d - 1], recv.at[d - 1], (s, lax.rem(z + d, reps)))
            for d in range(1, reps)
        ]

    up_copies = gather_copies(gathered, ag_send, ag_recv)
    for copy in up_copies:
        copy.start()

    @pl.when(has_other)
    def _():
        to_rest.start()

    @pl.when(helped)
    def _():
        to_share.wait_recv()
        for copy in spread_copies:
            copy.start()

    def assemble(buffer):
        for j in range(reps):
            full[j * block:(j + 1) * block, :] = buffer[j][:block].astype(F32)
        return full[...].astype(BF16)

    own_base = boxes
    near_base = 2 * boxes * (1 - parity)
    far_base = 2 * boxes * parity
    head = reps * piece
    to_near.wait_recv()

    def pick(chunk, _):
        columns = pl.ds(pl.multiple_of(chunk * wide, wide), wide)
        ramp = ramp_ref[...]
        row = jnp.concatenate([lists[entry:entry + 1, columns] for entry in range(slots)], axis=1)
        spots = one_hot(row - own_base, boxes, ramp) + one_hot(row - near_base, boxes, ramp)
        values = dot(window[:, :2 * boxes], stack(spots))
        for entry in range(slots):
            picked[entry, :, columns] = values[:, entry * wide:(entry + 1) * wide].astype(BF16)
        return 0

    first_part = 1
    lax.fori_loop(0, first_part, pick, 0)

    for copy in up_copies:
        copy.wait_recv()
    coarse_here[...] = jnp.concatenate(
        [assemble(gathered), jnp.zeros((coarse_here.shape[0] - rows, parents), BF16)], axis=0)
    coarse_window[:, :parents] = coarse_here[...]
    coarse_near = remote(
        coarse_here, coarse_window.at[:, pl.ds(parents, parents)], cw_send.at[0], cw_recv.at[0], (mate, z))
    coarse_far = remote(
        coarse_here, coarse_window.at[:, pl.ds(2 * parents, parents)], cw_send.at[1], cw_recv.at[1], (other, z))
    coarse_near.start()

    @pl.when(has_other)
    def _():
        coarse_far.start()

    lax.fori_loop(first_part, chunks, pick, 0)

    def coarse():
        coarse_near.wait_recv()

        @pl.when(has_other)
        def _():
            coarse_far.wait_recv()

        total = jnp.zeros((rows, parents), F32)
        row = jnp.concatenate([coarse_lists[entry:entry + 1, :] for entry in range(slots)], axis=1)
        ramp = lax.broadcasted_iota(jnp.int32, (parents, slots * parents), 0)
        place = [
            jnp.where(ramp == row - base, 1.0, 0.0).astype(BF16)
            for base in (own_base // children, near_base // children, far_base // children)
        ]
        values = dot(coarse_window[:rows, :], stack(place)).astype(BF16)
        for entry in range(slots):
            total += dot(far_ops[entry], values[:, entry * parents:(entry + 1) * parents])
        for j, value in enumerate(blocks_of(coarse_scale * total, reps, block, held)):
            coarse_sums[0, j] = value.astype(BF16)

    def move_right(chunk, ways, j):
        _, buffer, _, send, recv, _, _ = ways
        return remote(buffer.at[chunk, j], buffer.at[chunk, j], send.at[chunk, j], recv.at[chunk, j], (s, z + 1))

    def move_left(chunk, ways, j):
        _, _, buffer, _, _, send, recv = ways
        return remote(buffer.at[chunk, j], buffer.at[chunk, j], send.at[chunk, j], recv.at[chunk, j], (s, z - 1))

    def forward_right(chunk, ways):
        mine, buffer = ways[0], ways[1]
        for j in reversed(range(1, reps)):
            @pl.when(j > z)
            def _(j=j):
                copy = move_right(chunk, ways, j)

                @pl.when(z > 0)
                def _():
                    copy.wait_recv()
                    buffer[chunk, j] = (buffer[chunk, j].astype(F32) + mine[chunk, j].astype(F32)).astype(BF16)

                @pl.when(z == 0)
                def _():
                    buffer[chunk, j] = mine[chunk, j]

                copy.start()

    def forward_left(chunk, ways):
        mine, buffer = ways[0], ways[2]
        for j in range(reps - 1):
            @pl.when(j < z)
            def _(j=j):
                copy = move_left(chunk, ways, j)

                @pl.when(z < reps - 1)
                def _():
                    copy.wait_recv()
                    buffer[chunk, j] = (buffer[chunk, j].astype(F32) + mine[chunk, j].astype(F32)).astype(BF16)

                @pl.when(z == reps - 1)
                def _():
                    buffer[chunk, j] = mine[chunk, j]

                copy.start()

    def finished(chunk, ways):
        mine, go_right, go_left = ways[:3]

        @pl.when(z > 0)
        def _():
            move_right(chunk, ways, z).wait_recv()

        @pl.when(z == 0)
        def _():
            go_right[chunk, z] = jnp.zeros(go_right.shape[2:], BF16)

        @pl.when(z < reps - 1)
        def _():
            move_left(chunk, ways, z).wait_recv()

        @pl.when(z == reps - 1)
        def _():
            go_left[chunk, z] = jnp.zeros(go_left.shape[2:], BF16)

        return mine[chunk, z].astype(F32) + go_right[chunk, z].astype(F32) + go_left[chunk, z].astype(F32)

    def settle(chunk, ways):
        for j in range(reps):
            @pl.when(j > z)
            def _(j=j):
                move_right(chunk, ways, j).wait_send()

            @pl.when(j < z)
            def _(j=j):
                move_left(chunk, ways, j).wait_send()

    fine_ways = (sums, right, left, rs_send, rs_recv, ls_send, ls_recv)
    coarse_ways = (coarse_sums, coarse_right, coarse_left, crs_send, crs_recv, cls_send, cls_recv)

    def coarse_step(t):
        @pl.when(t == z)
        def _():
            forward_right(0, coarse_ways)

        @pl.when(t == reps - 1 - z)
        def _():
            forward_left(0, coarse_ways)

    def step(t):
        coarse_step(t - 1)

        @pl.when(jnp.logical_and(t >= z, t - z < chunks))
        def _():
            forward_right(t - z, fine_ways)

        back = reps - 1 - z

        @pl.when(jnp.logical_and(t >= back, t - back < chunks))
        def _():
            forward_left(t - back, fine_ways)

    def translate(t, _):
        @pl.when(whole_in)
        def _():
            pick_first(t, 0)

        columns = pl.ds(pl.multiple_of(t * wide, wide), wide)
        ramp = ramp_ref[...]
        total = jnp.zeros((rows, wide), F32)
        row = jnp.concatenate([lists[entry:entry + 1, columns] for entry in range(slots)], axis=1)
        values = dot(window[:, 2 * boxes + head:], stack(one_hot(row - far_base - head, boxes - head, ramp)))
        for entry in range(slots):
            source = values[:, entry * wide:(entry + 1) * wide] + picked[entry, :, columns].astype(F32)
            total += dot(far_ops[entry], source.astype(BF16))
        for j, value in enumerate(blocks_of(total, reps, block, held)):
            sums[t, j] = value.astype(BF16)
        step(t)

        @pl.when(jnp.logical_and(t == 0, jnp.logical_not(helped)))
        def _():
            coarse()

        return 0

    loads[2].wait()

    @pl.when(whole_in)
    def _():
        to_first.wait_recv()

    def pick_first(chunk, _):
        columns = pl.ds(pl.multiple_of(chunk * wide, wide), wide)
        row = jnp.concatenate([lists[entry:entry + 1, columns] for entry in range(slots)], axis=1)
        values = dot(window[:, 2 * boxes:2 * boxes + head], stack(one_hot(row - far_base, head, ramp_ref[...])))
        for entry in range(slots):
            part = values[:, entry * wide:(entry + 1) * wide] + picked[entry, :, columns].astype(F32)
            picked[entry, :, columns] = part.astype(BF16)
        return 0

    @pl.when(helped)
    def _():
        coarse()
        for copy in spread_copies:
            copy.wait_recv()
        lax.fori_loop(0, chunks, pick_first, 0)

    @pl.when(has_other)
    def _():
        to_rest.wait_recv()

    lax.fori_loop(0, chunks, translate, 0)

    check_copies = gather_copies(checks, ck_send, ck_recv)
    for t in range(chunks, chunks + reps - 1):
        step(t)
        if t == max(chunks, reps - 1):
            checks[z] = finished(0, coarse_ways).astype(BF16)
            for copy in check_copies:
                copy.start()

    for copy in check_copies:
        copy.wait_recv()
    check = assemble(checks)
    loads[3].wait()
    term = jnp.concatenate(
        [dot(down_raw[...], check), jnp.zeros((children * (held - block), parents), F32)], axis=0)
    for child, value in enumerate(by_child(term, children)):
        top = value[:block].astype(BF16)
        columns = pl.ds(child * parents, parents)
        high[:, columns] = top
        low[:, columns] = (value[:block] - top.astype(F32)).astype(BF16)

    def place(chunk, _):
        columns = pl.ds(pl.multiple_of(chunk * wide, wide), wide)
        parent = lax.broadcasted_iota(jnp.int32, (parents, wide), 0) * children
        box = lax.broadcasted_iota(jnp.int32, (parents, wide), 1) + chunk * wide
        spots = stack([
            jnp.where(parent == box - child, 1.0, 0.0).astype(BF16) for child in range(children)
        ])
        spread[:, columns] = dot(high[...], spots) + dot(low[...], spots)
        return 0

    lax.fori_loop(0, chunks, place, 0)

    def finish(chunk, _):
        columns = pl.ds(pl.multiple_of(chunk * wide, wide), wide)
        out[:, columns] = (finished(chunk, fine_ways)[:block] + spread[:, columns]).astype(BF16)
        settle(chunk, fine_ways)
        return 0

    lax.fori_loop(0, chunks, finish, 0)
    settle(0, coarse_ways)
    for copy in up_copies + check_copies + [to_near, coarse_near]:
        copy.wait_send()

    @pl.when(has_other)
    def _():
        to_rest.wait_send()

    @pl.when(helps)
    def _():
        to_share.wait_send()

    @pl.when(whole_out)
    def _():
        to_first.wait_send()

    @pl.when(helped)
    def _():
        for copy in spread_copies:
            copy.wait_send()

    @pl.when(has_other)
    def _():
        coarse_far.wait_send()


def local(spaces, reps, leaf_density, upward_ops, far_ops, downward_ops, fine_lists, coarse_lists):
    rows, boxes = leaf_density.shape
    children, block, _ = upward_ops.shape
    slots = far_ops.shape[0]
    parents = boxes // children
    wide = 256 if boxes % 256 == 0 else boxes
    chunks = boxes // wide
    piece = 128 if boxes >= 256 * reps else boxes // (2 * reps)
    by_row = [ops.transpose(1, 0, 2).reshape(block * children, rows) for ops in (upward_ops, downward_ops)]
    held = -(-block // 16) * 16
    padded = -(-rows // 16) * 16
    vm, dma = pltpu.VMEM, pltpu.SemaphoreType.DMA
    anywhere = pl.BlockSpec(memory_space=pl.ANY)
    inside = pl.BlockSpec(memory_space=vm)
    moving = vm((chunks, reps, held, wide), BF16)
    coarse_moving = vm((1, reps, held, parents), BF16)
    return pl.pallas_call(
        functools.partial(kernel, spaces, reps, wide, piece, block),
        out_shape=jax.ShapeDtypeStruct((block, boxes), BF16),
        in_specs=[anywhere] * 4 + [inside] * 2,
        out_specs=inside,
        scratch_shapes=[
            vm((rows, 3 * boxes), BF16),
            vm((block * children, rows), BF16), vm(far_ops.shape, BF16), vm((block * children, rows), BF16),
            vm(upward_ops.shape, BF16),
            vm((slots, rows, boxes), BF16), vm((min(256, boxes), slots * wide), BF16),
            moving, moving, moving,
            vm((reps, held, parents), BF16), vm((padded, parents), BF16), vm((padded, 3 * parents), BF16),
            coarse_moving, coarse_moving, coarse_moving,
            vm((reps, held, parents), BF16), vm((rows, parents), F32),
            vm((block, boxes), BF16), vm((block, boxes), BF16), vm((block, boxes), F32),
            dma((4,)), dma((4,)), dma((4,)), dma((reps - 1,)), dma((reps - 1,)), dma((2,)), dma((2,)),
            dma((reps - 1,)), dma((reps - 1,)), dma((reps - 1,)), dma((reps - 1,)),
        ] + [dma((chunks, reps))] * 4 + [dma((1, reps))] * 4,
        compiler_params=pltpu.CompilerParams(
            collective_id=0, has_side_effects=True, vmem_limit_bytes=56 * 2**20),
    )(leaf_density, by_row[0], far_ops, by_row[1], fine_lists, coarse_lists)


def solution(mesh):
    return jax.shard_map(
        functools.partial(local, mesh.shape["space"], mesh.shape["rep"]),
        mesh=mesh,
        in_specs=(
            P(None, "space"),
            P(None, "rep", None),
            P("rep", None, None),
            P(None, "rep", None),
            P("rep", "space"),
            P("rep", "space"),
        ),
        out_specs=P("rep", "space"),
        check_vma=False,
    )
```
